128 devices in a mesh: pp: 4 (over x_lo, core), ep: 32 (over z, x_hi, y).
Axes of the slice: x: 4 (x_hi: 2, x_lo: 2; x = x_hi * 2 + x_lo), y: 4, z: 4, core: 2. Of those that a mesh axis runs over, the one named last changes fastest.
Arguments:
- layer_input: bfloat16 [4, 4096, 2048], P('pp', 'ep'), may hold values from -6 to 6
- out_grad: bfloat16 [4, 4096, 2048], P('pp', 'ep'), may hold values from -1.5 to 1.5
- expert_ids: int32 [4, 4096, 8], P('pp', 'ep'), may hold values from 0 to 63, all different within a row; in each aligned block of 128 rows (0 to 127, 128 to 255, ..., all dimensions but the last counted through in order) at most 24 rows name the same one
- combine: float32 [4, 4096, 8], P('pp', 'ep'), may hold values from 0.05 to 1
- w_gate: bfloat16 [4, 64, 2048, 768], P('pp', 'ep'), may hold values from -0.125 to 0.125
- w_up: bfloat16 [4, 64, 2048, 768], P('pp', 'ep'), may hold values from -0.125 to 0.125
- w_down: bfloat16 [4, 64, 768, 2048], P('pp', 'ep'), may hold values from -0.21875 to 0.21875
Outputs:
- sent_grad: bfloat16 [4, 4096, 2048], P('pp', 'ep')
- combine_grad: bfloat16 [4, 4096, 8], P('pp', 'ep')
The draws below stay inside these ranges and needn't reach their ends.
Inputs may be any that keep to these rules, and one draw needn't show every extreme that they name: `expert_ids`: the 8 ids of a token differ. Within the rows of one device no expert is named more than 24 times, and in some device's rows some expert is named exactly 24 times.
All inputs are finite; a program needn't handle non-finite values.
Results may differ from the reference program's by a relative error of at most 0.011.
Values may be sent and summed in bfloat16 or wider, within the bound.
A program may use at most 128 MiB of HBM per device.

```python
import math
import jax
import jax.numpy as jnp
import numpy as np
from jax import lax

D = 2048
F = 768
EXP_DEV = 2
TOP = 8
TOK_DEV = 128
EXPERTS = 64
TOKENS = 4096
CAP = 24
SECTIONS = 4
N_PP = 4
N_EP = 32


def level_of(key, extent, shards, low, largest):
    loudness, own = 1.0, jax.random.fold_in(key, 6)
    for position, shards_of in shards:
        draws = jnp.exp(jax.random.uniform(jax.random.fold_in(own, position), (shards_of,), jnp.float32, low / len(shards), largest / len(shards)))
        loudness = loudness * jnp.repeat(draws, extent[position] // shards_of).reshape([-1 if axis == position else 1 for axis in range(len(extent))])
    return loudness


def deal_out(key, own, number, rows, count, top, limit, slope):
    ranking = jax.random.permutation(key, count)
    crowded, common = portions_of(count, rows * top, limit, slope, True), portions_of(count, rows * top, limit, slope, False)
    places = jnp.arange(count)

    def named(tallies, offset_by):
        used = int((tallies > 0).sum())
        fixed = max(1, used // 4)
        passed = fixed + (places - fixed + offset_by * (used - fixed)) % max(1, count - fixed)
        return jnp.zeros((count,), jnp.int32).at[ranking[jnp.where(places < fixed, places, passed)]].set(jnp.asarray(tallies, jnp.int32))

    tallies = jnp.where(number % 4 == 0, named(crowded, number // 4), named(common, number - number // 4 - 1))
    mixed = jax.random.permutation(jax.random.fold_in(own, 3), count)
    giver, receiver = mixed[0:count // 2 * 2:2], mixed[1:count // 2 * 2:2]
    margin = jnp.minimum(tallies[giver] - 1, limit - tallies[receiver]) // 2
    margin = jnp.where((giver == ranking[0]) | (receiver == ranking[0]) | (tallies[receiver] == 0), 0, jnp.maximum(margin, 0))
    passed = jax.random.randint(jax.random.fold_in(own, 4), (count // 2,), 0, 1 << 20) % (margin + 1)
    tallies = tallies.at[giver].add(-passed).at[receiver].add(passed)
    labels = jnp.searchsorted(jnp.cumsum(tallies), jnp.arange(rows * top), side="right").astype(jnp.int32)
    grid = labels.reshape(top, rows).T
    grid = grid[jax.random.permutation(jax.random.fold_in(own, 1), rows)]
    offset_by = jax.random.randint(jax.random.fold_in(own, 2), (rows, 1), 0, top)
    return jnp.take_along_axis(grid, (jnp.arange(top)[None, :] + offset_by) % top, axis=1)


def portions_of(number_of, total, limit, skew, full):
    weights = [(1 << 20) // math.isqrt(grade ** skew) + 1 for grade in range(1, number_of + 1)]
    largest = limit if full else min(limit, max(-(-total // number_of), total * weights[0] // sum(weights)))
    least = 1 if total - largest >= number_of - 1 else 0
    holding, surplus = [largest] + [least] * (number_of - 1), total - largest - least * (number_of - 1)
    while surplus > 0:
        free = [i for i in range(1, number_of) if holding[i] < largest] or [i for i in range(1, number_of) if holding[i] < limit]
        whole, left = sum([weights[i] for i in free]), surplus
        for i in free:
            extra = min(limit - holding[i], max(1, left * weights[i] // whole), surplus)
            holding[i] = holding[i] + extra
            surplus = surplus - extra
    return np.array(holding)


def scatter_about(key, shape, width, reach, shards=(), kind=jnp.bfloat16):
    factor_of = level_of(key, shape, shards, -0.22, 0.18) if shards else 1.0
    entries = jax.random.normal(key, shape, jnp.float32) * width * factor_of
    return jnp.minimum(jnp.maximum(entries, -reach), reach).astype(kind)


def setup_inputs(seed: int = 0) -> dict:
    key_of = jax.random.split(jax.random.key(seed), 8)
    layer_input = scatter_about(key_of[0], (SECTIONS, TOKENS, D), 1.0, 6.0, ((0, 4), (1, 32)))
    out_grad = scatter_about(key_of[1], (SECTIONS, TOKENS, D), 0.25, 1.5, ((0, 4), (1, 32)))
    expert_ids_keys = jax.random.split(jax.random.fold_in(key_of[2], 1), SECTIONS * TOKENS // TOK_DEV)
    expert_ids_turns = jax.random.permutation(jax.random.fold_in(key_of[2], 3), SECTIONS * TOKENS // TOK_DEV)
    expert_ids = jax.vmap(lambda own, number: deal_out(jax.random.fold_in(key_of[2], 2), own, number, TOK_DEV, EXPERTS, TOP, CAP, 2))(expert_ids_keys, expert_ids_turns).reshape((SECTIONS, TOKENS, TOP))
    combine = jnp.clip(jnp.exp(math.log(1.0) - 2.9957323 * jax.random.uniform(key_of[3], (SECTIONS, TOKENS, TOP), jnp.float32) ** level_of(key_of[3], (SECTIONS, TOKENS, TOP), ((0, 4), (1, 32)), -0.2, 0.2)), 0.05, 1.0)
    w_gate = scatter_about(key_of[4], (SECTIONS, EXPERTS, D, F), D ** -0.5, 0.125, ((0, 4), (1, 32)))
    w_up = scatter_about(key_of[5], (SECTIONS, EXPERTS, D, F), D ** -0.5, 0.125, ((0, 4), (1, 32)))
    w_down = scatter_about(key_of[6], (SECTIONS, EXPERTS, F, D), F ** -0.5, 0.21875, ((0, 4), (1, 32)))
    return dict(layer_input=layer_input, out_grad=out_grad, expert_ids=expert_ids, combine=combine, w_gate=w_gate, w_up=w_up, w_down=w_down)


def slot_table(ids_block):
    flat = ids_block.reshape(-1).astype(jnp.int32)
    onehot = (flat[:, None] == jnp.arange(EXPERTS, dtype=jnp.int32)[None, :]).astype(jnp.int32)
    ranks = jnp.sum(jnp.cumsum(onehot, axis=0) * onehot, axis=1) - 1
    return (flat * CAP + ranks).astype(jnp.int32)


def dispatch(rows, slots):
    count = slots.shape[0]
    source = jnp.full((EXPERTS * CAP,), rows.shape[0], jnp.int32)
    source = source.at[slots].set((jnp.arange(count, dtype=jnp.int32) // TOP).astype(jnp.int32))
    padded = jnp.concatenate([rows, jnp.zeros((1, rows.shape[1]), rows.dtype)], axis=0)
    return padded[source]


def expert_work(rows_in, grads_in, gate_w, up_w, down_w):
    rows_f = rows_in.astype(jnp.float32)
    grads_f = grads_in.astype(jnp.float32)
    gate_pre = jnp.einsum("secd,edf->secf", rows_f, gate_w.astype(jnp.float32))
    up_value = jnp.einsum("secd,edf->secf", rows_f, up_w.astype(jnp.float32))
    sigma = jax.nn.sigmoid(gate_pre)
    active = gate_pre * sigma
    hidden = (active * up_value).astype(jnp.bfloat16)
    expert_out = jnp.einsum("secf,efd->secd", hidden.astype(jnp.float32), down_w.astype(jnp.float32))
    score = jnp.sum(expert_out * grads_f, axis=-1).astype(jnp.bfloat16)
    hidden_grad = jnp.einsum("secd,efd->secf", grads_f, down_w.astype(jnp.float32))
    gate_grad = (hidden_grad * up_value * sigma * (1.0 + gate_pre * (1.0 - sigma))).astype(jnp.bfloat16)
    up_grad = (hidden_grad * active).astype(jnp.bfloat16)
    row_grad = jnp.einsum("secf,edf->secd", gate_grad.astype(jnp.float32), gate_w.astype(jnp.float32))
    row_grad = row_grad + jnp.einsum("secf,edf->secd", up_grad.astype(jnp.float32), up_w.astype(jnp.float32))
    return row_grad.astype(jnp.bfloat16), score


def combine_rows(back_rows, back_scores, slots, weights):
    picked = back_rows[slots].reshape(TOK_DEV, TOP, D).astype(jnp.float32)
    grad = jnp.sum(weights[:, :, None] * picked, axis=1).astype(jnp.bfloat16)
    return grad, back_scores[slots].reshape(TOK_DEV, TOP)


def reference(layer_input, out_grad, expert_ids, combine, w_gate, w_up, w_down):
    grads_all = []
    scores_all = []
    for section_idx in range(N_PP):
        slots = jax.vmap(slot_table)(expert_ids[section_idx].reshape(N_EP, TOK_DEV, TOP))
        send_rows = jax.vmap(dispatch)(layer_input[section_idx].reshape(N_EP, TOK_DEV, D), slots)
        send_grads = jax.vmap(dispatch)(out_grad[section_idx].reshape(N_EP, TOK_DEV, D), slots)
        send_rows = send_rows.reshape(N_EP, N_EP, EXP_DEV, CAP, D).transpose(1, 0, 2, 3, 4)
        send_grads = send_grads.reshape(N_EP, N_EP, EXP_DEV, CAP, D).transpose(1, 0, 2, 3, 4)
        gate_w = w_gate[section_idx].reshape(N_EP, EXP_DEV, D, F)
        up_w = w_up[section_idx].reshape(N_EP, EXP_DEV, D, F)
        down_w = w_down[section_idx].reshape(N_EP, EXP_DEV, F, D)

        def per_device(items):
            return expert_work(items[0], items[1], items[2], items[3], items[4])

        row_grad, score = lax.map(per_device, (send_rows, send_grads, gate_w, up_w, down_w))
        back_rows = row_grad.transpose(1, 0, 2, 3, 4).reshape(N_EP, EXPERTS * CAP, D)
        back_scores = score.transpose(1, 0, 2, 3).reshape(N_EP, EXPERTS * CAP)
        weights = combine[section_idx].reshape(N_EP, TOK_DEV, TOP)
        grad, scores = jax.vmap(combine_rows)(back_rows, back_scores, slots, weights)
        grads_all.append(grad.reshape(TOKENS, D))
        scores_all.append(scores.reshape(TOKENS, TOP))
    input_grad = jnp.stack(grads_all, axis=0)
    sent_grad = jnp.roll(input_grad, -1, axis=0)
    return sent_grad, jnp.stack(scores_all, axis=0)
```

```python
import functools

import jax
import jax.numpy as jnp
from jax import lax
from jax.experimental import pallas as pl
from jax.experimental.pallas import tpu as pltpu
from jax.sharding import PartitionSpec as P

MESH = pl.DeviceIdType.MESH
LINE = 4
ORDER = (0, -1, 1, 2)
BF16 = jnp.bfloat16
F32 = jnp.float32
ROWS, GRADS = 0, 1


def kernel(
    tok, cap, width, hidden_units,
    rows_in, grads_in, meta_in, gate_w, up_w, down_w,
    out_ref, cg_ref,
    blocks, metas, staged, arrived, returned, near, far, final,
    sel_s, wsel_s, wg, wu, wd, gg_s, ug_s, score_s, score_acc, score_r, cg_s, cg_r,
    x_send, x_recv, ag_send, ag_recv, meta_send, meta_recv, own_sem, w_sem,
    fwd_send, fwd_recv, ret_send, ret_recv, ret_own, sc_send, sc_recv, cg_send, cg_recv,
    rs_send, rs_recv, fin_send, fin_recv,
):
    slot = 2 * cap
    group = LINE * slot
    half = tok // 2
    cols = width // 2
    pair = 2 * tok
    per_expert = LINE * group
    pp, ep = lax.axis_index("pp"), lax.axis_index("ep")
    z, xh, y = ep // 8, (ep // 4) % 2, ep % 4
    line, cross = (z, y), (y, z)
    inputs = (rows_in, grads_in)

    def wrap(v):
        return lax.rem(v + LINE, LINE)

    def device(p, line_at, x_at, cross_at, section=None):
        z_at, y_at = (line_at, cross_at) if p == ROWS else (cross_at, line_at)
        return {"pp": pp if section is None else section, "ep": z_at * 8 + x_at * 4 + y_at}

    def remote(src, dst, send, recv, to):
        return pltpu.make_async_remote_copy(
            src_ref=src, dst_ref=dst, send_sem=send, recv_sem=recv, device_id=to, device_id_type=MESH
        )

    def place(p, line_at, x_at, part=None):
        start = ((p * LINE + line_at) * 2 + x_at) * tok
        if part is None:
            return blocks.at[pl.ds(pl.multiple_of(start, tok), tok), :]
        return blocks.at[pl.ds(pl.multiple_of(start + part * half, half), half), :]

    before, after = lax.rem(pp + 3, 4), lax.rem(pp + 1, 4)
    peers = [device(ROWS, wrap(z + o), x_at, y) for o in ORDER for x_at in (xh, 1 - xh)][1:]
    peers += [device(GRADS, wrap(y + o), x_at, z) for o in ORDER[1:] for x_at in (xh, 1 - xh)]
    peers += [device(ROWS, z, x_at, y, s) for x_at in (xh, 1 - xh) for s in (before, after)]
    barrier = pltpu.get_barrier_semaphore()
    for peer in peers:
        pl.semaphore_signal(barrier, inc=1, device_id=peer, device_id_type=MESH)
    pl.semaphore_wait(barrier, len(peers))

    def x_copy(p, part):
        rows = pl.ds(part * half, half)
        return remote(
            inputs[p].at[rows, :], place(p, line[p], xh, part), x_send.at[p, part], x_recv.at[p, part],
            device(p, line[p], 1 - xh, cross[p]),
        )

    def x_wait(p, part):
        remote(
            inputs[p].at[pl.ds(part * half, half), :], place(p, line[p], 1 - xh, part),
            x_send.at[p, part], x_recv.at[p, part], device(p, line[p], 1 - xh, cross[p]),
        ).wait_recv()

    def ag_part(d, k):
        return (d + k) % 2 if k < 2 else d

    def ag_copy(p, q, d, k):
        step = 1 - 2 * d
        part = ag_part(d, k)
        x_at = xh if q == 0 else 1 - xh
        at = line[p] if k < 2 else wrap(line[p] - step)
        dst = place(p, at, x_at, part)
        src = inputs[p].at[pl.ds(part * half, half), :] if q == 0 and k < 2 else dst
        return remote(
            src, dst, ag_send.at[p, q, d, k], ag_recv.at[p, q, d, k],
            device(p, wrap(line[p] + step), xh, cross[p]),
        )

    def ag_wait(p, q, d, k):
        step = 1 - 2 * d
        x_at = xh if q == 0 else 1 - xh
        at = wrap(line[p] - step) if k < 2 else wrap(line[p] + 2)
        dst = place(p, at, x_at, ag_part(d, k))
        remote(
            dst, dst, ag_send.at[p, q, d, k], ag_recv.at[p, q, d, k],
            device(p, wrap(line[p] + step), xh, cross[p]),
        ).wait_recv()

    def meta_copy(p, i, q):
        return remote(
            meta_in, metas.at[p, line[p], xh], meta_send.at[p, i, q], meta_recv.at[p, i, q],
            device(p, wrap(line[p] + ORDER[i]), xh if q == 0 else 1 - xh, cross[p]),
        )

    def meta_wait(p, i, q):
        remote(
            meta_in, metas.at[p, wrap(line[p] - ORDER[i]), xh if q == 0 else 1 - xh],
            meta_send.at[p, i, q], meta_recv.at[p, i, q],
            device(p, wrap(line[p] + ORDER[i]), xh if q == 0 else 1 - xh, cross[p]),
        ).wait_recv()

    others = [(i, q) for i in range(LINE) for q in range(2) if (i, q) != (0, 0)]
    paths = (ROWS, GRADS)
    for p in paths:
        for i, q in others:
            meta_copy(p, i, q).start()
    for p in paths:
        for part in range(2):
            x_copy(p, part).start()
    for k in range(2):
        for p in paths:
            for d in range(2):
                ag_copy(p, 0, d, k).start()
    own = []
    for p in paths:
        own.append(pltpu.make_async_copy(inputs[p], place(p, line[p], xh), own_sem.at[p]))
        own[-1].start()
        metas[p, line[p], xh] = meta_in[...]

    def weights(e):
        return [
            pltpu.make_async_copy(src.at[e], dst, w_sem.at[i])
            for i, (src, dst) in enumerate(((gate_w, wg), (up_w, wu), (down_w, wd)))
        ]

    for copy in weights(0):
        copy.start()
    for p in paths:
        for i, q in others:
            meta_wait(p, i, q)

    def expert_numbers(p):
        row = lax.broadcasted_iota(jnp.int32, (8, tok), 0)
        e, across = row // LINE, (row + cross[p]) % LINE
        if p == ROWS:
            return 16 * z + 8 * xh + 2 * across + e
        return 16 * across + 8 * xh + 2 * y + e

    earlier = (
        lax.broadcasted_iota(jnp.int32, (tok, tok), 0) < lax.broadcasted_iota(jnp.int32, (tok, tok), 1)
    ).astype(F32).astype(BF16)
    rank_no = lax.broadcasted_iota(jnp.int32, (cap, tok), 0).astype(F32)
    nothing = jnp.zeros((cap, tok), F32)

    for p in paths:
        numbers = expert_numbers(p).astype(F32)

        def build(i, carry, p=p, numbers=numbers):
            at = wrap(line[p] + jnp.where(i == 0, 0, jnp.where(i == 1, -1, i - 1)))
            found, weight, rank = [], [], []
            for h in range(2):
                meta = metas[p, at, h]
                member = jnp.zeros((8, tok), F32)
                share = jnp.zeros((8, tok), F32)
                for k in range(8):
                    same = meta[k : k + 1, :] == numbers
                    member = member + jnp.where(same, 1.0, 0.0)
                    share = share + jnp.where(same, meta[8 + k : 9 + k, :], 0.0)
                before_it = jnp.dot(member.astype(BF16), earlier, preferred_element_type=F32)
                rank.append(jnp.where(member > 0.0, before_it, -1.0))
                weight.append(share)
            hot, hot_w = [], []
            for row in range(8):
                for h in range(2):
                    hit = rank[h][row : row + 1, :] == rank_no
                    one = jnp.where(hit, 1.0, 0.0)
                    scaled = jnp.where(hit, weight[h][row : row + 1, :], 0.0)
                    hot.append(jnp.concatenate([one, nothing] if h == 0 else [nothing, one], axis=1))
                    hot_w.append(jnp.concatenate([scaled, nothing] if h == 0 else [nothing, scaled], axis=1))
            sel_s[p, i] = jnp.concatenate(hot, axis=0).astype(BF16)
            wsel_s[p, i] = jnp.concatenate(hot_w, axis=0).T.astype(BF16)
            return carry

        lax.fori_loop(0, LINE, build, 0)

    def arrived_at(p, e, from_cross, at):
        y_src, z_src = (from_cross, at) if p == ROWS else (at, from_cross)
        start = ((y_src * LINE) + z_src) * slot + (p * 2 + e) * per_expert
        return arrived.at[pl.ds(pl.multiple_of(start, 16), slot), :]

    def fwd_copy(p, e, j, i):
        at = wrap(line[p] + ORDER[i])
        return remote(
            staged.at[pl.ds((((p * 3 + j - 1) * 2 + e) * LINE + i) * slot, slot), :],
            arrived_at(p, e, cross[p], at), fwd_send.at[p, e, j - 1, i], fwd_recv.at[p, e, j - 1, i],
            device(p, line[p], xh, wrap(cross[p] + j)),
        )

    def fwd_wait(p, e, j, i):
        dst = arrived_at(p, e, wrap(cross[p] - j), wrap(line[p] + ORDER[i]))
        remote(
            dst, dst, fwd_send.at[p, e, j - 1, i], fwd_recv.at[p, e, j - 1, i],
            device(p, line[p], xh, wrap(cross[p] + j)),
        ).wait_recv()

    tile = 512

    def select(p, i):
        at = wrap(line[p] + ORDER[i])
        start = pl.multiple_of((p * LINE + at) * pair, pair)

        @pl.loop(0, width // tile)
        def _(n):
            lanes = pl.ds(pl.multiple_of(n * tile, tile), tile)
            picked = jnp.dot(
                sel_s[p, i], blocks[pl.ds(start, pair), lanes], preferred_element_type=F32
            ).astype(BF16)
            for e in range(2):
                for j in range(LINE):
                    part = picked[(e * LINE + j) * slot : (e * LINE + j + 1) * slot]
                    if j == 0:
                        arrived_at(p, e, cross[p], at)[:, lanes] = part
                    else:
                        first = (((p * 3 + j - 1) * 2 + e) * LINE + i) * slot
                        staged[pl.ds(first, slot), lanes] = part

    far_first = (2, 1, 3)

    def send_selected(e, i):
        for j in far_first:
            for p in paths:
                fwd_copy(p, e, j, i).start()

    for p in paths:
        for d in range(2):
            ag_wait(p, 0, d, 0)
            ag_copy(p, 0, d, 2).start()
    for part in range(2):
        for p in paths:
            x_wait(p, part)
            ag_copy(p, 1, part, 0).start()
    for p in paths:
        for d in range(2):
            ag_copy(p, 1, d, 1).start()
    for p in paths:
        own[p].wait()
        select(p, 0)
    send_selected(0, 0)
    for p in paths:
        for d in range(2):
            ag_wait(p, 1, d, 0)
            ag_copy(p, 1, d, 2).start()
    for i in (1, 2):
        for p in paths:
            for q in range(2):
                ag_wait(p, q, i - 1, 1)
            select(p, i)
        send_selected(0, i)
    for p in paths:
        for q in range(2):
            for d in range(2):
                ag_wait(p, q, d, 2)
        select(p, 3)
    send_selected(0, 3)
    for i in range(LINE):
        send_selected(1, i)
    for p in paths:
        for part in range(2):
            x_copy(p, part).wait_send()
        for q in range(2):
            for d in range(2):
                for k in range(3):
                    ag_copy(p, q, d, k).wait_send()
        for i, q in others:
            meta_copy(p, i, q).wait_send()

    def grad_rows(p, e, j):
        start = e * per_expert + wrap(cross[p] + j) * group
        return blocks.at[pl.ds(pl.multiple_of(start, 16), group), pl.ds(p * cols, cols)]

    def ret_copy(p, e, j):
        return remote(
            grad_rows(p, e, j), returned.at[p, e, LINE - j], ret_send.at[p, e, j - 1], ret_recv.at[p, e, j - 1],
            device(p, line[p], xh, wrap(cross[p] + j)),
        )

    def ret_wait(p, e, j):
        dst = returned.at[p, e, LINE - j]
        remote(
            dst, dst, ret_send.at[p, e, j - 1], ret_recv.at[p, e, j - 1],
            device(p, line[p], xh, wrap(cross[p] + j)),
        ).wait_recv()

    def own_return(p, e):
        return pltpu.make_async_copy(grad_rows(p, e, 0), returned.at[p, e, 0], ret_own.at[p, e])

    transposed = (((1,), (1,)), ((), ()))
    f_tile = 256
    d_tile = 256
    low = lax.broadcasted_iota(jnp.int32, (per_expert, 128), 1) < 64

    def expert(e):
        for copy in weights(e):
            copy.wait()
        for i in range(LINE):
            for p in paths:
                for j in far_first:
                    fwd_wait(p, e, j, i)
        row_at = pl.ds(e * per_expert, per_expert)
        grad_at = pl.ds((2 + e) * per_expert, per_expert)

        @pl.loop(0, hidden_units // f_tile)
        def _(n):
            units = pl.ds(pl.multiple_of(n * f_tile, f_tile), f_tile)
            gate = jnp.dot(arrived[row_at, :], wg[:, units], preferred_element_type=F32)
            up = jnp.dot(arrived[row_at, :], wu[:, units], preferred_element_type=F32)
            back = lax.dot_general(arrived[grad_at, :], wd[units, :], transposed, preferred_element_type=F32)
            sigma = jax.nn.sigmoid(gate)
            active = gate * sigma
            hidden = (active * up).astype(BF16).astype(F32)
            term = hidden * back
            gg_s[:, units] = (back * up * sigma * (1.0 + gate * (1.0 - sigma))).astype(BF16)
            ug_s[:, units] = (back * active).astype(BF16)
            term = term[:, :128] + term[:, 128:]

            @pl.when(n == 0)
            def _():
                score_acc[...] = term

            @pl.when(n > 0)
            def _():
                score_acc[...] += term

        score = jnp.broadcast_to(jnp.sum(score_acc[...], axis=1, keepdims=True), (per_expert, 128))
        if e == 0:
            score_s[...] = score.astype(BF16)
        else:
            score_s[...] = jnp.where(low, score_s[...].astype(F32), score).astype(BF16)

        for p in paths:

            @pl.loop(0, cols // d_tile)
            def _(n, p=p):
                lanes = pl.ds(pl.multiple_of(p * cols + n * d_tile, d_tile), d_tile)
                grad = lax.dot_general(gg_s[...], wg[lanes, :], transposed, preferred_element_type=F32)
                grad = grad + lax.dot_general(ug_s[...], wu[lanes, :], transposed, preferred_element_type=F32)
                grad = grad.astype(BF16)
                if p == ROWS:
                    blocks[pl.ds(e * per_expert, per_expert), lanes] = grad
                else:
                    for y_src in range(LINE):
                        for z_src in range(LINE):
                            to = e * per_expert + (z_src * LINE + y_src) * slot
                            source = (y_src * LINE + z_src) * slot
                            blocks[pl.ds(to, slot), lanes] = grad[source : source + slot]

            for j in far_first:
                ret_copy(p, e, j).start()
            own_return(p, e).start()

    def score_rows(j):
        return score_s.at[pl.ds(pl.multiple_of(wrap(y + j) * group, 16), group), :]

    def score_copy(j):
        return remote(
            score_rows(j), score_r.at[LINE - j], sc_send.at[j - 1], sc_recv.at[j - 1],
            device(ROWS, z, xh, wrap(y + j)),
        )

    expert(0)
    for copy in weights(1):
        copy.start()
    expert(1)
    for j in far_first:
        score_copy(j).start()
    score_r[0] = score_rows(0)[...]
    for p in paths:
        for e in range(2):
            for j in far_first:
                for i in range(LINE):
                    fwd_copy(p, e, j, i).wait_send()

    def partial_at(p, at, x_at, part=None):
        start = (at * 2 + x_at) * tok
        lanes = pl.ds(p * cols, cols)
        if part is None:
            return staged.at[pl.ds(pl.multiple_of(start, tok), tok), lanes]
        return staged.at[pl.ds(pl.multiple_of(start + part * half, half), half), lanes]

    def combine(p, i):
        at = wrap(line[p] + ORDER[i])
        take = pl.ds(pl.multiple_of(at * slot, 16), slot)
        gathered = jnp.concatenate([returned[p, e, j, take, :] for e in range(2) for j in range(LINE)], axis=0)
        rows = pl.ds(pl.multiple_of(at * pair, pair), pair)
        for n in range(cols // tile):
            staged[rows, pl.ds(p * cols + n * tile, tile)] = jnp.dot(
                wsel_s[p, i], gathered[:, n * tile : (n + 1) * tile], preferred_element_type=F32
            ).astype(BF16)

    def rs_copy(p, q, d, k):
        step = 1 - 2 * d
        x_at = xh if q == 0 else 1 - xh
        at = wrap(line[p] + 2) if k == 0 else wrap(line[p] + step)
        part = 1 - d if k == 1 else d
        dst = far.at[p, q, d] if k == 0 else near.at[p, q, d, part]
        return remote(
            partial_at(p, at, x_at, part), dst, rs_send.at[p, q, d, k], rs_recv.at[p, q, d, k],
            device(p, wrap(line[p] + step), xh, cross[p]),
        )

    def fin_copy(p, q):
        x_at = xh if q == 0 else 1 - xh
        return remote(
            partial_at(p, line[p], x_at), final.at[q, p], fin_send.at[p, q], fin_recv.at[p, q],
            device(p, line[p], x_at, cross[p], before),
        )

    def cg_copy(i, q):
        return remote(
            cg_s.at[i, q], cg_r.at[i, q], cg_send.at[i, q], cg_recv.at[i, q],
            device(ROWS, wrap(z + ORDER[i]), xh if q == 0 else 1 - xh, y),
        )

    for p in paths:
        for e in range(2):
            for j in far_first:
                ret_wait(p, e, j)
            own_return(p, e).wait()
        combine(p, 3)
        for q in (1, 0):
            for d in range(2):
                rs_copy(p, q, d, 0).start()
        for i in (1, 2):
            combine(p, i)
            for q in (1, 0):
                rs_copy(p, q, 2 - i, 1).start()
        combine(p, 0)

    for j in far_first:
        score_copy(j).wait_recv()
    lane = lax.broadcasted_iota(jnp.int32, (slot, 128), 1)
    numbers = expert_numbers(ROWS).astype(F32)
    for i in range(LINE):
        at = wrap(z + ORDER[i])
        take = pl.ds(pl.multiple_of(at * slot, 16), slot)
        spread = []
        for e in range(2):
            for j in range(LINE):
                mine = (lane // 64 == e) & (lane % 8 == e * LINE + j)
                spread.append(jnp.where(mine, score_r[j, take, :].astype(F32), 0.0))
        spread = jnp.concatenate(spread, axis=0).T.astype(BF16)
        by_expert = jnp.dot(spread, sel_s[ROWS, i], preferred_element_type=F32)
        by_expert = by_expert[0:8] + by_expert[64:72]
        for q in range(2):
            x_at = xh if q == 0 else 1 - xh
            ids = metas[ROWS, at, x_at][0:8]
            mine = jnp.where(x_at == 0, by_expert[:, :tok], by_expert[:, tok:])
            total = jnp.zeros((8, tok), F32)
            for row in range(8):
                total = total + jnp.where(ids == numbers[row : row + 1], mine[row : row + 1], 0.0)
            cg_s[i, q] = total
            if (i, q) != (0, 0):
                cg_copy(i, q).start()

    for q in (1, 0):
        for p in paths:
            for d in range(2):
                rs_copy(p, q, d, 0).wait_recv()
                step = 1 - 2 * d
                x_at = xh if q == 0 else 1 - xh
                mid = partial_at(p, wrap(line[p] + step), x_at, d)
                mid[...] = (mid[...].astype(F32) + far[p, q, d].astype(F32)).astype(BF16)
                rs_copy(p, q, d, 2).start()
    for q in (1, 0):
        for p in paths:
            for d in range(2):
                for k in (1, 2):
                    rs_copy(p, q, d, k).wait_recv()
            x_at = xh if q == 0 else 1 - xh
            mine = partial_at(p, line[p], x_at)
            for part in range(2):
                rows = pl.ds(part * half, half)
                mine[rows, :] = (
                    mine[rows, :].astype(F32) + near[p, q, 0, part].astype(F32) + near[p, q, 1, part].astype(F32)
                ).astype(BF16)
            fin_copy(p, q).start()

    total = cg_s[0, 0]
    for i, q in others:
        cg_copy(i, q).wait_recv()
        total = total + cg_r[i, q]
    cg_ref[...] = total
    for p in paths:
        for q in range(2):
            fin_copy(p, q).wait_recv()
        out_ref[:, pl.ds(p * cols, cols)] = (final[0, p].astype(F32) + final[1, p].astype(F32)).astype(BF16)

    for p in paths:
        for e in range(2):
            for j in far_first:
                ret_copy(p, e, j).wait_send()
        for q in range(2):
            for d in range(2):
                for k in range(3):
                    rs_copy(p, q, d, k).wait_send()
            fin_copy(p, q).wait_send()
    for j in far_first:
        score_copy(j).wait_send()
    for i, q in others:
        cg_copy(i, q).wait_send()


def on_device(layer_input, out_grad, expert_ids, combine, w_gate, w_up, w_down):
    tok, width = layer_input.shape[1:]
    hidden_units = w_gate.shape[3]
    experts = w_gate.shape[1] * lax.axis_size("ep")
    cap = 3 * tok * expert_ids.shape[2] // (2 * experts)
    slot = 2 * cap
    per_expert = LINE * LINE * slot
    cols = width // 2
    meta = jnp.concatenate([expert_ids[0].astype(F32).T, combine[0].T], axis=0)
    vmem, hbm = pl.BlockSpec(memory_space=pltpu.VMEM), pl.BlockSpec(memory_space=pl.ANY)
    dma = pltpu.SemaphoreType.DMA
    grad, scores = pl.pallas_call(
        functools.partial(kernel, tok, cap, width, hidden_units),
        out_shape=(jax.ShapeDtypeStruct((tok, width), BF16), jax.ShapeDtypeStruct((8, tok), F32)),
        in_specs=[hbm, hbm, vmem, hbm, hbm, hbm],
        out_specs=(vmem, vmem),
        scratch_shapes=[
            pltpu.VMEM((2 * LINE * 2 * tok, width), BF16),
            pltpu.VMEM((2, LINE, 2, 16, tok), F32),
            pltpu.VMEM((2 * 3 * 2 * LINE * slot, width), BF16),
            pltpu.VMEM((2 * 2 * per_expert, width), BF16),
            pltpu.VMEM((2, 2, LINE, LINE * slot, cols), BF16),
            pltpu.VMEM((2, 2, 2, 2, tok // 2, cols), BF16),
            pltpu.VMEM((2, 2, 2, tok // 2, cols), BF16),
            pltpu.VMEM((2, 2, tok, cols), BF16),
            pltpu.VMEM((2, LINE, 8 * slot, 2 * tok), BF16),
            pltpu.VMEM((2, LINE, 2 * tok, 8 * slot), BF16),
            pltpu.VMEM((width, hidden_units), BF16),
            pltpu.VMEM((width, hidden_units), BF16),
            pltpu.VMEM((hidden_units, width), BF16),
            pltpu.VMEM((per_expert, hidden_units), BF16),
            pltpu.VMEM((per_expert, hidden_units), BF16),
            pltpu.VMEM((per_expert, 128), BF16),
            pltpu.VMEM((per_expert, 128), F32),
            pltpu.VMEM((LINE, LINE * slot, 128), BF16),
            pltpu.VMEM((LINE, 2, 8, tok), F32),
            pltpu.VMEM((LINE, 2, 8, tok), F32),
            dma((2, 2)), dma((2, 2)),
            dma((2, 2, 2, 3)), dma((2, 2, 2, 3)),
            dma((2, LINE, 2)), dma((2, LINE, 2)),
            dma((2,)), dma((3,)),
            dma((2, 2, 3, LINE)), dma((2, 2, 3, LINE)),
            dma((2, 2, 3)), dma((2, 2, 3)), dma((2, 2)),
            dma((3,)), dma((3,)),
            dma((LINE, 2)), dma((LINE, 2)),
            dma((2, 2, 2, 3)), dma((2, 2, 2, 3)),
            dma((2, 2)), dma((2, 2)),
        ],
        compiler_params=pltpu.CompilerParams(
            collective_id=0, has_side_effects=True, vmem_limit_bytes=63 << 20
        ),
        cost_estimate=pl.CostEstimate(
            flops=10 * 2 * per_expert * width * hidden_units, bytes_accessed=24 << 20, transcendentals=0
        ),
        name="routed_backward",
    )(layer_input[0], out_grad[0], meta, w_gate[0], w_up[0], w_down[0])
    return grad[None], scores.T.astype(BF16)[None]


def solution(mesh):
    return jax.shard_map(
        on_device,
        mesh=mesh,
        in_specs=(
            P("pp", "ep", None),
            P("pp", "ep", None),
            P("pp", "ep", None),
            P("pp", "ep", None),
            P("pp", "ep", None, None),
            P("pp", "ep", None, None),
            P("pp", "ep", None, None),
        ),
        out_specs=(P("pp", "ep", None), P("pp", "ep", None)),
        check_vma=False,
    )
```

```python
import functools

import jax
import jax.numpy as jnp
from jax import lax
from jax.experimental import pallas as pl
from jax.experimental.pallas import tpu as pltpu
from jax.sharding import PartitionSpec as P

MESH = pl.DeviceIdType.MESH
LINE = 4
BF16 = jnp.bfloat16
F32 = jnp.float32
ROWS, GRADS = 0, 1


def kernel(
    tok, cap, width, hidden_units,
    rows_in, grads_in, ids_in, share_in, gate_w, up_w, down_w,
    out_ref, cg_ref,
    blocks, metas, staged, arrived, returned, near, far, beside, final,
    sel_s, wsel_s, wg, wu, wd, gg_s, ug_s, score_0, score_s, score_acc, score_r, cg_s, cg_r,
    block_send, x_recv, xn_recv, ag_recv, ag_far, meta_send, meta_recv, own_sem, w_sem,
    fwd_send, fwd_recv, ret_send, ret_recv, ret_own, sc_send, sc_recv, cg_send, cg_recv,
    rs_send, rs_recv, far_recv, beside_recv, fin_send, fin_recv,
):
    slot = 2 * cap
    group = LINE * slot
    half = tok // 2
    cols = width // 2
    pair = 2 * tok
    per_expert = LINE * group
    pp, ep = lax.axis_index("pp"), lax.axis_index("ep")
    z, xh, y = ep // 8, (ep // 4) % 2, ep % 4
    line, cross = (z, y), (y, z)
    inputs = (rows_in, grads_in)

    def wrap(v):
        return lax.rem(v + LINE, LINE)

    def member(p, i):
        c = line[p]
        return (c, (c // 2) * 2 + 1 - c % 2, wrap(c + 2), 3 - c)[i]

    def column(q):
        return xh if q == 0 else 1 - xh

    def chunk(p, s):
        at = line[p] // 2 if s % 2 == 0 else 1 - line[p] // 2
        return column(s // 2), at

    chunks = range(4)

    def device(p, line_at, x_at, cross_at, section=None):
        z_at, y_at = (line_at, cross_at) if p == ROWS else (cross_at, line_at)
        return {"pp": pp if section is None else section, "ep": z_at * 8 + x_at * 4 + y_at}

    def remote(src, dst, send, recv, to):
        return pltpu.make_async_remote_copy(
            src_ref=src, dst_ref=dst, send_sem=send, recv_sem=recv, device_id=to, device_id_type=MESH
        )

    def drain(ref, sem):
        pltpu.make_async_copy(ref, ref, sem).wait()

    def meta_at(p, line_at, x_at):
        return (p * LINE + line_at) * 2 + x_at

    def place(p, line_at, x_at, part=None):
        start = ((p * 2 + x_at) * LINE + line_at) * tok
        if part is None:
            return blocks.at[pl.ds(pl.multiple_of(start, tok), tok), :]
        return blocks.at[pl.ds(pl.multiple_of(start + part * half, half), half), :]

    before, after = lax.rem(pp + 3, 4), lax.rem(pp + 1, 4)
    peers = [device(ROWS, member(ROWS, i), column(q), y) for i in range(LINE) for q in range(2)][1:]
    peers += [device(GRADS, member(GRADS, i), column(q), z) for i in range(1, LINE) for q in range(2)]
    peers += [device(ROWS, z, x_at, y, s) for x_at in (xh, 1 - xh) for s in (before, after)]
    barrier = pltpu.get_barrier_semaphore()
    for peer in peers:
        pl.semaphore_signal(barrier, inc=1, device_id=peer, device_id_type=MESH)
    pl.semaphore_wait(barrier, len(peers))

    def own_half(p, part):
        return inputs[p].at[pl.ds(pl.multiple_of(part * half, half), half), :]

    def x_copy(p, part):
        return remote(
            own_half(p, part), place(p, line[p], xh, part), block_send, x_recv.at[p],
            device(p, line[p], 1 - xh, cross[p]),
        )

    def x_wait(p):
        drain(place(p, line[p], 1 - xh), x_recv.at[p])

    def xn_copy(p, d, k):
        dst = place(p, wrap(line[p] - (1 - 2 * d)), xh, ag_part(d, k))
        return remote(dst, dst, block_send, xn_recv.at[p, d, k], device(p, line[p], 1 - xh, cross[p]))

    def xn_wait(p, d, k):
        drain(place(p, wrap(line[p] - (1 - 2 * d)), 1 - xh, ag_part(d, k)), xn_recv.at[p, d, k])

    def ag_part(d, k):
        return lax.rem(d + k, 2) if k < 2 else d

    def ag_copy(p, q, d, k):
        step = 1 - 2 * d
        part = ag_part(d, k)
        x_at = xh if q == 0 else 1 - xh
        at = line[p] if k < 2 else wrap(line[p] - step)
        dst = place(p, at, x_at, part)
        src = own_half(p, part) if q == 0 and k < 2 else dst
        sem = ag_recv.at[p, d, k] if k < 2 else ag_far.at[p, q]
        return remote(src, dst, block_send, sem, device(p, wrap(line[p] + step), xh, cross[p]))

    def ag_wait(p, d, k):
        drain(place(p, wrap(line[p] - (1 - 2 * d)), xh, ag_part(d, k)), ag_recv.at[p, d, k])

    def ag_wait_far(p, q):
        drain(place(p, wrap(line[p] + 2), column(q)), ag_far.at[p, q])

    def meta_copy(p, i, q):
        mine = metas.at[meta_at(p, line[p], xh)]
        return remote(mine, mine, meta_send, meta_recv, device(p, member(p, i), column(q), cross[p]))

    others = [(i, q) for i in range(LINE) for q in range(2) if (i, q) != (0, 0)]
    paths = (ROWS, GRADS)
    for p in paths:
        metas[meta_at(p, line[p], xh), 0:8] = ids_in[...].astype(F32)
        metas[meta_at(p, line[p], xh), 8:16] = share_in[...]
        for i, q in others:
            meta_copy(p, i, q).start()
    for p in paths:
        for part in range(2):
            x_copy(p, part).start()
    for k in range(2):
        for p in paths:
            for d in range(2):
                ag_copy(p, 0, d, k).start()
    own = []
    for p in paths:
        own.append(pltpu.make_async_copy(inputs[p], place(p, line[p], xh), own_sem.at[p]))
        own[-1].start()

    def weights(e):
        return [
            pltpu.make_async_copy(src.at[e], dst, w_sem.at[i])
            for i, (src, dst) in enumerate(((gate_w, wg), (up_w, wu), (down_w, wd)))
        ]

    for copy in weights(0):
        copy.start()
    all_metas = metas.at[pl.ds(0, 2 * len(others))]
    drain(all_metas, meta_recv)

    def expert_numbers(p):
        row = lax.broadcasted_iota(jnp.int32, (8, tok), 0)
        e, across = row // LINE, (row + cross[p]) % LINE
        if p == ROWS:
            return 16 * z + 8 * xh + 2 * across + e
        return 16 * across + 8 * xh + 2 * y + e

    earlier = (
        lax.broadcasted_iota(jnp.int32, (tok, tok), 0) < lax.broadcasted_iota(jnp.int32, (tok, tok), 1)
    ).astype(F32).astype(BF16)
    rank_no = lax.broadcasted_iota(jnp.int32, (cap, tok), 0).astype(F32)
    nothing = jnp.zeros((cap, tok), F32)

    for p in paths:
        numbers = expert_numbers(p).astype(F32)

        def build(i, carry, p=p, numbers=numbers):
            x_at = lax.rem(xh + i // 2, 2)
            own_pair = line[p] // 2
            first_line = 2 * lax.rem(own_pair + i % 2, 2)
            weight, rank = [], []
            for h in range(2):
                meta = metas[meta_at(p, first_line + h, x_at)]
                named = jnp.zeros((8, tok), F32)
                share = jnp.zeros((8, tok), F32)
                for k in range(8):
                    same = meta[k : k + 1, :] == numbers
                    named = named + jnp.where(same, 1.0, 0.0)
                    share = share + jnp.where(same, meta[8 + k : 9 + k, :], 0.0)
                before_it = jnp.dot(named.astype(BF16), earlier, preferred_element_type=F32)
                rank.append(jnp.where(named > 0.0, before_it, -1.0))
                weight.append(share)
            hot, hot_w = [], []
            for row in range(8):
                for h in range(2):
                    hit = rank[h][row : row + 1, :] == rank_no
                    one = jnp.where(hit, 1.0, 0.0)
                    scaled = jnp.where(hit, weight[h][row : row + 1, :], 0.0)
                    hot.append(jnp.concatenate([one, nothing] if h == 0 else [nothing, one], axis=1))
                    hot_w.append(jnp.concatenate([scaled, nothing] if h == 0 else [nothing, scaled], axis=1))
            sel_s[p, i] = jnp.concatenate(hot, axis=0).astype(BF16)
            wsel_s[p, i] = jnp.concatenate(hot_w, axis=0).T.astype(BF16)
            return carry

        lax.fori_loop(0, LINE, build, 0)

    def arrived_at(p, e, from_cross, x_at, pair_at):
        start = (p * 2 + e) * per_expert + ((x_at * LINE + from_cross) * 2 + pair_at) * slot
        return arrived.at[pl.ds(pl.multiple_of(start, 16), slot), :]

    def fwd_copy(p, e, j, s):
        return remote(
            staged.at[pl.ds((((p * 3 + j - 1) * 2 + e) * 4 + s) * slot, slot), :],
            arrived_at(p, e, cross[p], *chunk(p, s)), fwd_send, fwd_recv.at[p, e],
            device(p, line[p], xh, wrap(cross[p] + j)),
        )

    tile = 512

    def select(p, s):
        x_at, pair_at = chunk(p, s)
        start = pl.multiple_of(((p * 2 + x_at) * 2 + pair_at) * pair, pair)

        @pl.loop(0, width // tile)
        def _(n):
            lanes = pl.ds(pl.multiple_of(n * tile, tile), tile)
            picked = jnp.dot(
                sel_s[p, s], blocks[pl.ds(start, pair), lanes], preferred_element_type=F32
            ).astype(BF16)
            for e in range(2):
                for j in range(LINE):
                    part = picked[(e * LINE + j) * slot : (e * LINE + j + 1) * slot]
                    if j == 0:
                        arrived_at(p, e, cross[p], x_at, pair_at)[:, lanes] = part
                    else:
                        first = (((p * 3 + j - 1) * 2 + e) * 4 + s) * slot
                        staged[pl.ds(first, slot), lanes] = part

    far_first = (2, 1, 3)

    def send_selected(p, e, s):
        for j in far_first:
            fwd_copy(p, e, j, s).start()

    near_way = [1 - line[p] % 2 for p in paths]
    far_way = [line[p] % 2 for p in paths]
    for p in paths:
        for d in (near_way[p], far_way[p]):
            ag_wait(p, d, 0)
            ag_copy(p, 0, d, 2).start()
            xn_copy(p, d, 0).start()
    for p in paths:
        ag_wait(p, near_way[p], 1)
        xn_copy(p, near_way[p], 1).start()
        own[p].wait()
        select(p, 0)
        for e in range(2):
            send_selected(p, e, 0)
    for p in paths:
        ag_wait(p, far_way[p], 1)
        xn_copy(p, far_way[p], 1).start()
        ag_wait_far(p, 0)
        select(p, 1)
        for e in range(2):
            send_selected(p, e, 1)
    for p in paths:
        x_wait(p)
        xn_wait(p, near_way[p], 0)
        ag_copy(p, 1, near_way[p], 2).start()
        xn_wait(p, near_way[p], 1)
        select(p, 2)
        send_selected(p, 0, 2)
    for p in paths:
        xn_wait(p, far_way[p], 0)
        ag_copy(p, 1, far_way[p], 2).start()
    for p in paths:
        xn_wait(p, far_way[p], 1)
        ag_wait_far(p, 1)
        select(p, 3)
        send_selected(p, 0, 3)
    for s in (2, 3):
        for p in paths:
            send_selected(p, 1, s)
    drain(blocks.at[pl.ds(0, 14 * tok), :], block_send)
    drain(all_metas, meta_send)

    def grad_rows(p, e, j, q):
        start = e * per_expert + wrap(cross[p] + j) * group + column(q) * (group // 2)
        return blocks.at[pl.ds(pl.multiple_of(start, 16), group // 2), pl.ds(p * cols, cols)]

    def ret_copy(p, e, j, q):
        return remote(
            grad_rows(p, e, j, q), returned.at[p, q, LINE - j, e], ret_send, ret_recv.at[p, q],
            device(p, line[p], xh, wrap(cross[p] + j)),
        )

    def own_return(p, e, q):
        return pltpu.make_async_copy(grad_rows(p, e, 0, q), returned.at[p, q, 0, e], ret_own.at[p, q])

    transposed = (((1,), (1,)), ((), ()))
    f_tile = 256
    d_tile = 256
    low = lax.broadcasted_iota(jnp.int32, (per_expert, 128), 1) < 64

    def reorder(value):
        return jnp.concatenate(
            [
                value[((x_at * LINE + b) * LINE + a) * cap : ((x_at * LINE + b) * LINE + a + 1) * cap]
                for x_at in range(2) for a in range(LINE) for b in range(LINE)
            ],
            axis=0,
        )

    def to_return(value, p):
        parts = []
        for dst in range(LINE):
            for x_at in range(2):
                for src in range(LINE):
                    y_at, z_at = (dst, src) if p == ROWS else (src, dst)
                    first = ((x_at * LINE + y_at) * LINE + z_at) * cap
                    parts.append(value[first : first + cap])
        return jnp.concatenate(parts, axis=0)

    def expert(e):
        for copy in weights(e):
            copy.wait()
        for p in paths:
            drain(arrived.at[pl.ds((p * 2 + e) * per_expert, 3 * group), :], fwd_recv.at[p, e])
        row_at = pl.ds(e * per_expert, per_expert)
        grad_at = pl.ds((2 + e) * per_expert, per_expert)

        @pl.loop(0, hidden_units // f_tile)
        def _(n):
            units = pl.ds(pl.multiple_of(n * f_tile, f_tile), f_tile)
            gate = jnp.dot(arrived[row_at, :], wg[:, units], preferred_element_type=F32)
            up = jnp.dot(arrived[row_at, :], wu[:, units], preferred_element_type=F32)
            back = lax.dot_general(arrived[grad_at, :], wd[units, :], transposed, preferred_element_type=F32)
            back = reorder(back)
            sigma = jax.nn.sigmoid(gate)
            active = gate * sigma
            hidden = (active * up).astype(BF16).astype(F32)
            term = hidden * back
            gg_s[:, units] = (back * up * sigma * (1.0 + gate * (1.0 - sigma))).astype(BF16)
            ug_s[:, units] = (back * active).astype(BF16)
            term = term[:, :128] + term[:, 128:]

            @pl.when(n == 0)
            def _():
                score_acc[...] = term

            @pl.when(n > 0)
            def _():
                score_acc[...] += term

        for p in paths:

            @pl.loop(0, cols // d_tile)
            def _(n, p=p):
                lanes = pl.ds(pl.multiple_of(p * cols + n * d_tile, d_tile), d_tile)
                grad = lax.dot_general(gg_s[...], wg[lanes, :], transposed, preferred_element_type=F32)
                grad = grad + lax.dot_general(ug_s[...], wu[lanes, :], transposed, preferred_element_type=F32)
                blocks[pl.ds(e * per_expert, per_expert), lanes] = to_return(grad, p).astype(BF16)

            for q in (1, 0):
                for j in far_first:
                    ret_copy(p, e, j, q).start()
                own_return(p, e, q).start()

        score = jnp.broadcast_to(jnp.sum(score_acc[...], axis=1, keepdims=True), (per_expert, 128))
        if e == 0:
            score_0[...] = score
        else:
            score_0[...] = jnp.where(low, score_0[...], score)

    def score_copy(j):
        return remote(
            score_s.at[wrap(y + j)], score_r.at[LINE - j], sc_send, sc_recv,
            device(ROWS, z, xh, wrap(y + j)),
        )

    expert(0)
    for copy in weights(1):
        copy.start()
    expert(1)
    blank = jnp.zeros((128 - slot, 128), F32)
    first = lax.broadcasted_iota(jnp.int32, (8, 128), 0) < 4
    for y_src in range(LINE):
        for t in range(4):
            start = ((t // 2 * LINE + y_src) * 2 + t % 2) * slot
            turned = jnp.concatenate([score_0[start : start + slot, :], blank], axis=0).T
            score_s[y_src, :, t * 128 : (t + 1) * 128] = jnp.where(first, turned[0:8], turned[64:72])
    for j in far_first:
        score_copy(j).start()
    score_r[0] = score_s[y]
    drain(staged, fwd_send)

    def partial_at(p, at, x_at, part=None):
        start = (x_at * LINE + at) * tok
        lanes = pl.ds(p * cols, cols)
        if part is None:
            return staged.at[pl.ds(pl.multiple_of(start, tok), tok), lanes]
        return staged.at[pl.ds(pl.multiple_of(start + part * half, half), half), lanes]

    def combine(p, s):
        x_at, pair_at = chunk(p, s)
        take = pl.ds(pl.multiple_of(pair_at * slot, 16), slot)
        gathered = jnp.concatenate([returned[p, s // 2, j, e, take, :] for e in range(2) for j in range(LINE)], axis=0)
        rows = pl.ds(pl.multiple_of((x_at * 2 + pair_at) * pair, pair), pair)
        for n in range(cols // tile):
            staged[rows, pl.ds(p * cols + n * tile, tile)] = jnp.dot(
                wsel_s[p, s], gathered[:, n * tile : (n + 1) * tile], preferred_element_type=F32
            ).astype(BF16)

    def rs_copy(p, d, k):
        step = 1 - 2 * d
        at = wrap(line[p] + 2) if k == 0 else wrap(line[p] + step)
        part = 1 - d if k == 1 else d
        dst = far.at[p, d] if k == 0 else near.at[p, 0, d, pl.ds(pl.multiple_of(part * half, half), half)]
        return remote(
            partial_at(p, at, xh, part), dst, rs_send, far_recv.at[p] if k == 0 else rs_recv.at[p, 0],
            device(p, wrap(line[p] + step), xh, cross[p]),
        )

    def rs_whole(p, d):
        step = 1 - 2 * d
        return remote(
            partial_at(p, wrap(line[p] + step), 1 - xh), near.at[p, 1, d], rs_send, rs_recv.at[p, 1],
            device(p, wrap(line[p] + step), xh, cross[p]),
        )

    def beside_copy(p):
        return remote(
            partial_at(p, wrap(line[p] + 2), 1 - xh), beside.at[p], rs_send, beside_recv.at[p],
            device(p, line[p], 1 - xh, cross[p]),
        )

    def fin_copy(p, q):
        x_at = xh if q == 0 else 1 - xh
        return remote(
            partial_at(p, line[p], x_at), final.at[q, p], fin_send, fin_recv,
            device(p, line[p], x_at, cross[p], before),
        )

    def cg_copy(i, q):
        return remote(
            cg_s.at[2 * i + q], cg_r.at[2 * i + q - 1], cg_send, cg_recv,
            device(ROWS, member(ROWS, i), column(q), y),
        )

    def sum_up(p, q):
        mine = partial_at(p, line[p], column(q))
        mine[...] = (
            mine[...].astype(F32) + near[p, q, 0].astype(F32) + near[p, q, 1].astype(F32)
        ).astype(BF16)

    def wait_returned(p, q):
        drain(returned.at[p, q, pl.ds(1, 3)], ret_recv.at[p, q])
        drain(returned.at[p, q, 0], ret_own.at[p, q])

    for p in paths:
        wait_returned(p, 1)
        combine(p, 3)
        beside_copy(p).start()
        rs_whole(p, near_way[p]).start()
        combine(p, 2)
        rs_whole(p, far_way[p]).start()
    for p in paths:
        wait_returned(p, 0)
        combine(p, 1)
        rs_copy(p, near_way[p], 1).start()
        drain(beside.at[p], beside_recv.at[p])
        mine = partial_at(p, wrap(line[p] + 2), xh)
        mine[...] = (mine[...].astype(F32) + beside[p].astype(F32)).astype(BF16)
        for d in range(2):
            rs_copy(p, d, 0).start()
        combine(p, 0)
        rs_copy(p, far_way[p], 1).start()
    for p in paths:
        drain(near.at[p, 1], rs_recv.at[p, 1])
        sum_up(p, 1)
        fin_copy(p, 1).start()

    drain(score_r.at[pl.ds(1, 3)], sc_recv)
    row = lax.broadcasted_iota(jnp.int32, (8, 128), 0)
    numbers = expert_numbers(ROWS).astype(F32)
    pad = jnp.zeros((128 - slot, pair), BF16)
    for s in chunks:
        x_at, pair_at = chunk(ROWS, s)
        take = pl.ds(pl.multiple_of((x_at * 2 + pair_at) * 128, 128), 128)
        by_expert = jnp.zeros((8, pair), F32)
        for j in range(LINE):
            tile_j = score_r[j, :, take]
            for e in range(2):
                block = e * LINE + j
                mine = jnp.where(row == block, tile_j, 0.0).astype(BF16)
                hot = jnp.concatenate([sel_s[ROWS, s, block * slot : (block + 1) * slot, :], pad], axis=0)
                by_expert = by_expert + jnp.dot(mine, hot, preferred_element_type=F32)
        for m in range(2):
            i, q = 2 * (s % 2) + m, s // 2
            ids = metas[meta_at(ROWS, member(ROWS, i), x_at), 0:8]
            mine = jnp.where(lax.rem(z + m, 2) == 0, by_expert[:, :tok], by_expert[:, tok:])
            total = jnp.zeros((8, tok), F32)
            for block in range(8):
                total = total + jnp.where(ids == numbers[block : block + 1], mine[block : block + 1], 0.0)
            cg_s[2 * i + q] = total
            if (i, q) != (0, 0):
                cg_copy(i, q).start()

    for p in paths:
        drain(far.at[p], far_recv.at[p])
        for d in range(2):
            mid = partial_at(p, wrap(line[p] + 1 - 2 * d), xh, d)
            mid[...] = (mid[...].astype(F32) + far[p, d].astype(F32)).astype(BF16)
            rs_copy(p, d, 2).start()
    for p in paths:
        drain(near.at[p, 0], rs_recv.at[p, 0])
        sum_up(p, 0)
        fin_copy(p, 0).start()

    drain(cg_r, cg_recv)
    total = cg_s[0]
    for i in range(len(others)):
        total = total + cg_r[i]
    cg_ref[...] = total.astype(BF16)
    drain(final, fin_recv)
    for p in paths:
        out_ref[:, pl.ds(p * cols, cols)] = (final[0, p].astype(F32) + final[1, p].astype(F32)).astype(BF16)

    drain(blocks.at[pl.ds(0, 6 * group), :], ret_send)
    drain(staged.at[pl.ds(0, 12 * tok), pl.ds(0, cols)], rs_send)
    drain(final, fin_send)
    drain(score_r.at[pl.ds(1, 3)], sc_send)
    drain(cg_r, cg_send)


def on_device(layer_input, out_grad, expert_ids, combine, w_gate, w_up, w_down):
    tok, width = layer_input.shape[1:]
    hidden_units = w_gate.shape[3]
    experts = w_gate.shape[1] * lax.axis_size("ep")
    cap = 3 * tok * expert_ids.shape[2] // (2 * experts)
    slot = 2 * cap
    per_expert = LINE * LINE * slot
    cols = width // 2
    vmem, hbm = pl.BlockSpec(memory_space=pltpu.VMEM), pl.BlockSpec(memory_space=pl.ANY)
    dma = pltpu.SemaphoreType.DMA
    grad, scores = pl.pallas_call(
        functools.partial(kernel, tok, cap, width, hidden_units),
        out_shape=(jax.ShapeDtypeStruct((tok, width), BF16), jax.ShapeDtypeStruct((8, tok), BF16)),
        in_specs=[hbm, hbm, vmem, vmem, hbm, hbm, hbm],
        out_specs=(vmem, vmem),
        scratch_shapes=[
            pltpu.VMEM((2 * LINE * 2 * tok, width), BF16),
            pltpu.VMEM((2 * LINE * 2, 16, tok), F32),
            pltpu.VMEM((2 * 3 * 2 * LINE * slot, width), BF16),
            pltpu.VMEM((2 * 2 * per_expert, width), BF16),
            pltpu.VMEM((2, 2, LINE, 2, 2 * slot, cols), BF16),
            pltpu.VMEM((2, 2, 2, tok, cols), BF16),
            pltpu.VMEM((2, 2, tok // 2, cols), BF16),
            pltpu.VMEM((2, tok, cols), BF16),
            pltpu.VMEM((2, 2, tok, cols), BF16),
            pltpu.VMEM((2, LINE, 8 * slot, 2 * tok), BF16),
            pltpu.VMEM((2, LINE, 2 * tok, 8 * slot), BF16),
            pltpu.VMEM((width, hidden_units), BF16),
            pltpu.VMEM((width, hidden_units), BF16),
            pltpu.VMEM((hidden_units, width), BF16),
            pltpu.VMEM((per_expert, hidden_units), BF16),
            pltpu.VMEM((per_expert, hidden_units), BF16),
            pltpu.VMEM((per_expert, 128), F32),
            pltpu.VMEM((LINE, 8, LINE * 128), F32),
            pltpu.VMEM((per_expert, 128), F32),
            pltpu.VMEM((LINE, 8, LINE * 128), F32),
            pltpu.VMEM((LINE * 2, 8, tok), F32),
            pltpu.VMEM((LINE * 2 - 1, 8, tok), F32),
            dma, dma((2,)), dma((2, 2, 2)), dma((2, 2, 2)), dma((2, 2)), dma, dma, dma((2,)), dma((3,)),
            dma, dma((2, 2)), dma, dma((2, 2)), dma((2, 2)), dma, dma, dma, dma,
            dma, dma((2, 2)), dma((2,)), dma((2,)), dma, dma,
        ],
        compiler_params=pltpu.CompilerParams(
            collective_id=0, has_side_effects=True, vmem_limit_bytes=63 << 20
        ),
        cost_estimate=pl.CostEstimate(
            flops=10 * 2 * per_expert * width * hidden_units, bytes_accessed=24 << 20, transcendentals=0
        ),
        name="routed_backward",
    )(layer_input[0], out_grad[0], expert_ids[0].T, combine[0].T, w_gate[0], w_up[0], w_down[0])
    return grad[None], scores.T[None]


def solution(mesh):
    return jax.shard_map(
        on_device,
        mesh=mesh,
        in_specs=(
            P("pp", "ep", None),
            P("pp", "ep", None),
            P("pp", "ep", None),
            P("pp", "ep", None),
            P("pp", "ep", None, None),
            P("pp", "ep", None, None),
            P("pp", "ep", None, None),
        ),
        out_specs=(P("pp", "ep", None), P("pp", "ep", None)),
        check_vma=False,
    )
```

```python
import functools

import jax
import jax.numpy as jnp
from jax import lax
from jax.experimental import pallas as pl
from jax.experimental.pallas import tpu as pltpu
from jax.sharding import PartitionSpec as P

MESH = pl.DeviceIdType.MESH
LINE = 4
BF16 = jnp.bfloat16
F32 = jnp.float32
ROWS, GRADS = 0, 1


def kernel(
    tok, cap, width, hidden_units,
    rows_in, grads_in, ids_in, share_in, gate_w, up_w, down_w,
    out_ref, cg_ref,
    blocks, early, metas, staged, arrived, returned, near, far, beside, final,
    sel_s, wsel_s, wg, wu, wd, gg_s, ug_s, score_0, score_s, score_acc, score_r, cg_s, cg_r,
    block_send, x_recv, xn_recv, ag_recv, ag_far, meta_send, meta_recv, own_sem, w_sem,
    fwd_send, fwd_recv, ret_send, ret_recv, ret_own, sc_send, sc_recv, cg_send, cg_recv,
    rs_send, rs_recv, far_recv, beside_recv, fin_send, fin_recv,
):
    slot = 2 * cap
    group = LINE * slot
    half = tok // 2
    cols = width // 2
    pair = 2 * tok
    per_expert = LINE * group
    part_rows = per_expert // 2
    pp, ep = lax.axis_index("pp"), lax.axis_index("ep")
    z, xh, y = ep // 8, (ep // 4) % 2, ep % 4
    line, cross = (z, y), (y, z)
    inputs = (rows_in, grads_in)

    def wrap(v):
        return lax.rem(v + LINE, LINE)

    def member(p, i):
        c = line[p]
        return (c, (c // 2) * 2 + 1 - c % 2, wrap(c + 2), 3 - c)[i]

    def column(q):
        return xh if q == 0 else 1 - xh

    def chunk(p, s):
        at = line[p] // 2 if s % 2 == 0 else 1 - line[p] // 2
        return column(s // 2), at

    chunks = range(4)

    def device(p, line_at, x_at, cross_at, section=None):
        z_at, y_at = (line_at, cross_at) if p == ROWS else (cross_at, line_at)
        return {"pp": pp if section is None else section, "ep": z_at * 8 + x_at * 4 + y_at}

    def remote(src, dst, send, recv, to):
        return pltpu.make_async_remote_copy(
            src_ref=src, dst_ref=dst, send_sem=send, recv_sem=recv, device_id=to, device_id_type=MESH
        )

    def drain(ref, sem):
        pltpu.make_async_copy(ref, ref, sem).wait()

    def meta_at(p, line_at, x_at):
        return (p * LINE + line_at) * 2 + x_at

    def place(p, line_at, x_at, part=None):
        start = ((p * 2 + x_at) * LINE + line_at) * tok
        if part is None:
            return blocks.at[pl.ds(pl.multiple_of(start, tok), tok), :]
        return blocks.at[pl.ds(pl.multiple_of(start + part * half, half), half), :]

    before, after = lax.rem(pp + 3, 4), lax.rem(pp + 1, 4)
    peers = [device(ROWS, member(ROWS, i), column(q), y) for i in range(LINE) for q in range(2)][1:]
    peers += [device(GRADS, member(GRADS, i), column(q), z) for i in range(1, LINE) for q in range(2)]
    peers += [device(ROWS, z, x_at, y, s) for x_at in (xh, 1 - xh) for s in (before, after)]
    barrier = pltpu.get_barrier_semaphore()
    for peer in peers:
        pl.semaphore_signal(barrier, inc=1, device_id=peer, device_id_type=MESH)
    pl.semaphore_wait(barrier, len(peers))

    def own_half(p, part):
        return inputs[p].at[pl.ds(pl.multiple_of(part * half, half), half), :]

    def x_copy(p, part):
        return remote(
            own_half(p, part), place(p, line[p], xh, part), block_send, x_recv.at[p],
            device(p, line[p], 1 - xh, cross[p]),
        )

    def x_wait(p):
        drain(place(p, line[p], 1 - xh), x_recv.at[p])

    def xn_copy(p, d, k):
        dst = place(p, wrap(line[p] - (1 - 2 * d)), xh, ag_part(d, k))
        return remote(dst, dst, block_send, xn_recv.at[p, d, k], device(p, line[p], 1 - xh, cross[p]))

    def xn_wait(p, d, k):
        drain(place(p, wrap(line[p] - (1 - 2 * d)), 1 - xh, ag_part(d, k)), xn_recv.at[p, d, k])

    def ag_part(d, k):
        return lax.rem(d + k, 2) if k < 2 else d

    def ag_copy(p, q, d, k):
        step = 1 - 2 * d
        part = ag_part(d, k)
        x_at = xh if q == 0 else 1 - xh
        at = line[p] if k < 2 else wrap(line[p] - step)
        dst = place(p, at, x_at, part)
        src = own_half(p, part) if q == 0 and k < 2 else dst
        sem = ag_recv.at[p, d, k] if k < 2 else ag_far.at[p, q]
        return remote(src, dst, block_send, sem, device(p, wrap(line[p] + step), xh, cross[p]))

    def ag_wait(p, d, k):
        drain(place(p, wrap(line[p] - (1 - 2 * d)), xh, ag_part(d, k)), ag_recv.at[p, d, k])

    def ag_wait_far(p, q):
        drain(place(p, wrap(line[p] + 2), column(q)), ag_far.at[p, q])

    def meta_copy(p, i, q):
        mine = metas.at[meta_at(p, line[p], xh)]
        return remote(mine, mine, meta_send, meta_recv, device(p, member(p, i), column(q), cross[p]))

    others = [(i, q) for i in range(LINE) for q in range(2) if (i, q) != (0, 0)]
    paths = (ROWS, GRADS)
    for p in paths:
        metas[meta_at(p, line[p], xh), 0:8] = ids_in[...].astype(F32)
        metas[meta_at(p, line[p], xh), 8:16] = share_in[...]
        for i, q in others:
            meta_copy(p, i, q).start()
    for p in paths:
        for part in range(2):
            x_copy(p, part).start()
    for k in range(2):
        for p in paths:
            for d in range(2):
                ag_copy(p, 0, d, k).start()
    own = []
    for p in paths:
        own.append(pltpu.make_async_copy(inputs[p], place(p, line[p], xh), own_sem.at[p]))
        own[-1].start()

    def weights(e):
        return [
            pltpu.make_async_copy(src.at[e], dst, w_sem.at[i])
            for i, (src, dst) in enumerate(((gate_w, wg), (up_w, wu), (down_w, wd)))
        ]

    for copy in weights(0):
        copy.start()
    all_metas = metas.at[pl.ds(0, 2 * len(others))]
    drain(all_metas, meta_recv)

    def expert_numbers(p):
        row = lax.broadcasted_iota(jnp.int32, (8, tok), 0)
        e, across = row // LINE, (row + cross[p]) % LINE
        if p == ROWS:
            return 16 * z + 8 * xh + 2 * across + e
        return 16 * across + 8 * xh + 2 * y + e

    earlier = (
        lax.broadcasted_iota(jnp.int32, (tok, tok), 0) < lax.broadcasted_iota(jnp.int32, (tok, tok), 1)
    ).astype(F32).astype(BF16)
    rank_no = lax.broadcasted_iota(jnp.int32, (cap, tok), 0).astype(F32)
    nothing = jnp.zeros((cap, tok), F32)

    for p in paths:
        numbers = expert_numbers(p).astype(F32)

        def build(i, carry, p=p, numbers=numbers):
            x_at = lax.rem(xh + i // 2, 2)
            own_pair = line[p] // 2
            first_line = 2 * lax.rem(own_pair + i % 2, 2)
            weight, rank = [], []
            for h in range(2):
                meta = metas[meta_at(p, first_line + h, x_at)]
                named = jnp.zeros((8, tok), F32)
                share = jnp.zeros((8, tok), F32)
                for k in range(8):
                    same = meta[k : k + 1, :] == numbers
                    named = named + jnp.where(same, 1.0, 0.0)
                    share = share + jnp.where(same, meta[8 + k : 9 + k, :], 0.0)
                before_it = jnp.dot(named.astype(BF16), earlier, preferred_element_type=F32)
                rank.append(jnp.where(named > 0.0, before_it, -1.0))
                weight.append(share)
            hot, hot_w = [], []
            for row in range(8):
                for h in range(2):
                    hit = rank[h][row : row + 1, :] == rank_no
                    one = jnp.where(hit, 1.0, 0.0)
                    scaled = jnp.where(hit, weight[h][row : row + 1, :], 0.0)
                    hot.append(jnp.concatenate([one, nothing] if h == 0 else [nothing, one], axis=1))
                    hot_w.append(jnp.concatenate([scaled, nothing] if h == 0 else [nothing, scaled], axis=1))
            sel_s[p, i] = jnp.concatenate(hot, axis=0).astype(BF16)
            wsel_s[p, i] = jnp.concatenate(hot_w, axis=0).T.astype(BF16)
            return carry

        lax.fori_loop(0, LINE, build, 0)

    def arrived_at(p, e, from_cross, x_at, pair_at):
        start = (p * 2 + e) * per_expert + ((x_at * LINE + from_cross) * 2 + pair_at) * slot
        return arrived.at[pl.ds(pl.multiple_of(start, 16), slot), :]

    def fwd_copy(p, e, j, s):
        return remote(
            staged.at[pl.ds((((p * 3 + j - 1) * 2 + e) * 4 + s) * slot, slot), :],
            arrived_at(p, e, cross[p], *chunk(p, s)), fwd_send, fwd_recv.at[p, e, s // 2],
            device(p, line[p], xh, wrap(cross[p] + j)),
        )

    tile = 512

    def select(p, s):
        x_at, pair_at = chunk(p, s)
        start = pl.multiple_of(((p * 2 + x_at) * 2 + pair_at) * pair, pair)

        @pl.loop(0, width // tile)
        def _(n):
            lanes = pl.ds(pl.multiple_of(n * tile, tile), tile)
            picked = jnp.dot(
                sel_s[p, s], blocks[pl.ds(start, pair), lanes], preferred_element_type=F32
            ).astype(BF16)
            for e in range(2):
                for j in range(LINE):
                    part = picked[(e * LINE + j) * slot : (e * LINE + j + 1) * slot]
                    if j == 0:
                        arrived_at(p, e, cross[p], x_at, pair_at)[:, lanes] = part
                    else:
                        first = (((p * 3 + j - 1) * 2 + e) * 4 + s) * slot
                        staged[pl.ds(first, slot), lanes] = part

    far_first = (2, 1, 3)

    def send_selected(p, e, s):
        for j in far_first:
            fwd_copy(p, e, j, s).start()

    def grad_rows(p, e, q, size, start):
        if (e, q) == (0, 0):
            return early.at[pl.ds(start, size), pl.ds(p * cols, cols)]
        base = {(0, 1): 0, (1, 1): 1, (1, 0): 2}[e, q] * part_rows
        return blocks.at[pl.ds(pl.multiple_of(base + start, 16), size), pl.ds(p * cols, cols)]

    def grads_for(p, e, q, j):
        return grad_rows(p, e, q, group // 2, pl.multiple_of(wrap(cross[p] + j) * (group // 2), 16))

    def ret_copy(p, e, j, q):
        return remote(
            grads_for(p, e, q, j), returned.at[p, q, LINE - j, e], ret_send, ret_recv.at[p, q],
            device(p, line[p], xh, wrap(cross[p] + j)),
        )

    def own_return(p, e, q):
        return pltpu.make_async_copy(grads_for(p, e, q, 0), returned.at[p, q, 0, e], ret_own.at[p, q])

    transposed = (((1,), (1,)), ((), ()))
    f_tile = 256
    d_tile = 256
    low = lax.broadcasted_iota(jnp.int32, (part_rows, 128), 1) < 64

    def turn(value):
        blocks_of = [value[(a * LINE + b) * cap : (a * LINE + b + 1) * cap] for b in range(LINE) for a in range(LINE)]
        return jnp.concatenate(blocks_of, axis=0)

    def expert(e, q):
        for p in paths:
            drain(arrived.at[pl.ds((p * 2 + e) * per_expert, 3 * group // 2), :], fwd_recv.at[p, e, q])
        offset = column(q) * part_rows
        row_at = pl.ds(pl.multiple_of(e * per_expert + offset, part_rows), part_rows)
        grad_at = pl.ds(pl.multiple_of((2 + e) * per_expert + offset, part_rows), part_rows)

        @pl.loop(0, hidden_units // f_tile)
        def _(n):
            units = pl.ds(pl.multiple_of(n * f_tile, f_tile), f_tile)
            gate = jnp.dot(arrived[row_at, :], wg[:, units], preferred_element_type=F32)
            up = jnp.dot(arrived[row_at, :], wu[:, units], preferred_element_type=F32)
            back = lax.dot_general(arrived[grad_at, :], wd[units, :], transposed, preferred_element_type=F32)
            back = turn(back)
            sigma = jax.nn.sigmoid(gate)
            active = gate * sigma
            hidden = (active * up).astype(BF16).astype(F32)
            term = hidden * back
            gg_s[:, units] = (back * up * sigma * (1.0 + gate * (1.0 - sigma))).astype(BF16)
            ug_s[:, units] = (back * active).astype(BF16)
            term = term[:, :128] + term[:, 128:]

            @pl.when(n == 0)
            def _():
                score_acc[...] = term

            @pl.when(n > 0)
            def _():
                score_acc[...] += term

        for p in paths:

            @pl.loop(0, cols // d_tile)
            def _(n, p=p):
                lanes = pl.ds(pl.multiple_of(p * cols + n * d_tile, d_tile), d_tile)
                grad = lax.dot_general(gg_s[...], wg[lanes, :], transposed, preferred_element_type=F32)
                grad = grad + lax.dot_general(ug_s[...], wu[lanes, :], transposed, preferred_element_type=F32)
                grad = (grad if p == ROWS else turn(grad)).astype(BF16)
                grad_rows(p, e, q, part_rows, 0)[:, pl.ds(pl.multiple_of(n * d_tile, d_tile), d_tile)] = grad

            for j in far_first:
                ret_copy(p, e, j, q).start()
            own_return(p, e, q).start()

        score = jnp.broadcast_to(jnp.sum(score_acc[...], axis=1, keepdims=True), (part_rows, 128))
        rows = pl.ds(pl.multiple_of(offset, part_rows), part_rows)
        if e == 0:
            score_0[rows, :] = score
        else:
            score_0[rows, :] = jnp.where(low, score_0[rows, :], score)

    near_way = [1 - line[p] % 2 for p in paths]
    far_way = [line[p] % 2 for p in paths]
    for p in paths:
        ag_wait(p, near_way[p], 0)
        ag_copy(p, 0, near_way[p], 2).start()
        xn_copy(p, near_way[p], 0).start()
        ag_wait(p, far_way[p], 0)
        ag_copy(p, 0, far_way[p], 2).start()
    for p in paths:
        ag_wait(p, near_way[p], 1)
        xn_copy(p, near_way[p], 1).start()
        own[p].wait()
        select(p, 0)
        send_selected(p, 0, 0)
    for p in paths:
        ag_wait(p, far_way[p], 1)
        ag_wait_far(p, 0)
        select(p, 1)
        send_selected(p, 0, 1)
    for s in (0, 1):
        for p in paths:
            send_selected(p, 1, s)
    for p in paths:
        x_wait(p)
        for k in range(2):
            xn_copy(p, far_way[p], k).start()
    for copy in weights(0):
        copy.wait()
    expert(0, 0)
    for p in paths:
        xn_wait(p, near_way[p], 0)
        ag_copy(p, 1, near_way[p], 2).start()
        xn_wait(p, near_way[p], 1)
        select(p, 2)
        send_selected(p, 0, 2)
    for p in paths:
        xn_wait(p, far_way[p], 0)
        ag_copy(p, 1, far_way[p], 2).start()
    for p in paths:
        xn_wait(p, far_way[p], 1)
        ag_wait_far(p, 1)
        select(p, 3)
        send_selected(p, 0, 3)
    for s in (2, 3):
        for p in paths:
            send_selected(p, 1, s)
    drain(blocks.at[pl.ds(0, 14 * tok), :], block_send)
    drain(all_metas, meta_send)

    def score_copy(j):
        return remote(
            score_s.at[wrap(y + j)], score_r.at[LINE - j], sc_send, sc_recv,
            device(ROWS, z, xh, wrap(y + j)),
        )

    expert(0, 1)
    for copy in weights(1):
        copy.start()
    for copy in weights(1):
        copy.wait()
    expert(1, 1)
    expert(1, 0)
    blank = jnp.zeros((128 - slot, 128), F32)
    first = lax.broadcasted_iota(jnp.int32, (8, 128), 0) < 4
    for y_src in range(LINE):
        for t in range(4):
            start = ((t // 2 * LINE + y_src) * 2 + t % 2) * slot
            turned = jnp.concatenate([score_0[start : start + slot, :], blank], axis=0).T
            score_s[y_src, :, t * 128 : (t + 1) * 128] = jnp.where(first, turned[0:8], turned[64:72])
    for j in far_first:
        score_copy(j).start()
    score_r[0] = score_s[y]
    drain(staged, fwd_send)

    def partial_at(p, at, x_at, part=None):
        start = (x_at * LINE + at) * tok
        lanes = pl.ds(p * cols, cols)
        if part is None:
            return staged.at[pl.ds(pl.multiple_of(start, tok), tok), lanes]
        return staged.at[pl.ds(pl.multiple_of(start + part * half, half), half), lanes]

    def combine(p, s):
        x_at, pair_at = chunk(p, s)
        take = pl.ds(pl.multiple_of(pair_at * slot, 16), slot)
        gathered = jnp.concatenate([returned[p, s // 2, j, e, take, :] for e in range(2) for j in range(LINE)], axis=0)
        rows = pl.ds(pl.multiple_of((x_at * 2 + pair_at) * pair, pair), pair)
        for n in range(cols // tile):
            staged[rows, pl.ds(p * cols + n * tile, tile)] = jnp.dot(
                wsel_s[p, s], gathered[:, n * tile : (n + 1) * tile], preferred_element_type=F32
            ).astype(BF16)

    def rs_copy(p, d, k):
        step = 1 - 2 * d
        at = wrap(line[p] + 2) if k == 0 else wrap(line[p] + step)
        part = 1 - d if k == 1 else d
        dst = far.at[p, d] if k == 0 else near.at[p, 0, d, pl.ds(pl.multiple_of(part * half, half), half)]
        return remote(
            partial_at(p, at, xh, part), dst, rs_send, far_recv.at[p] if k == 0 else rs_recv.at[p, 0],
            device(p, wrap(line[p] + step), xh, cross[p]),
        )

    def rs_whole(p, d):
        step = 1 - 2 * d
        return remote(
            partial_at(p, wrap(line[p] + step), 1 - xh), near.at[p, 1, d], rs_send, rs_recv.at[p, 1],
            device(p, wrap(line[p] + step), xh, cross[p]),
        )

    def beside_copy(p):
        return remote(
            partial_at(p, wrap(line[p] + 2), 1 - xh), beside.at[p], rs_send, beside_recv.at[p],
            device(p, line[p], 1 - xh, cross[p]),
        )

    def fin_copy(p, q):
        x_at = xh if q == 0 else 1 - xh
        return remote(
            partial_at(p, line[p], x_at), final.at[q, p], fin_send, fin_recv,
            device(p, line[p], x_at, cross[p], before),
        )

    def cg_copy(i, q):
        return remote(
            cg_s.at[2 * i + q], cg_r.at[2 * i + q - 1], cg_send, cg_recv,
            device(ROWS, member(ROWS, i), column(q), y),
        )

    def sum_up(p, q):
        mine = partial_at(p, line[p], column(q))
        mine[...] = (
            mine[...].astype(F32) + near[p, q, 0].astype(F32) + near[p, q, 1].astype(F32)
        ).astype(BF16)

    def wait_returned(p, q):
        drain(returned.at[p, q, pl.ds(1, 3)], ret_recv.at[p, q])
        drain(returned.at[p, q, 0], ret_own.at[p, q])

    for p in paths:
        wait_returned(p, 1)
        combine(p, 3)
        beside_copy(p).start()
        rs_whole(p, near_way[p]).start()
        combine(p, 2)
        rs_whole(p, far_way[p]).start()
    for p in paths:
        wait_returned(p, 0)
        combine(p, 1)
        rs_copy(p, near_way[p], 1).start()
        drain(beside.at[p], beside_recv.at[p])
        mine = partial_at(p, wrap(line[p] + 2), xh)
        mine[...] = (mine[...].astype(F32) + beside[p].astype(F32)).astype(BF16)
        for d in range(2):
            rs_copy(p, d, 0).start()
        combine(p, 0)
        rs_copy(p, far_way[p], 1).start()
    for p in paths:
        drain(near.at[p, 1], rs_recv.at[p, 1])
        sum_up(p, 1)
        fin_copy(p, 1).start()

    drain(score_r.at[pl.ds(1, 3)], sc_recv)
    row = lax.broadcasted_iota(jnp.int32, (8, 128), 0)
    numbers = expert_numbers(ROWS).astype(F32)
    pad = jnp.zeros((128 - slot, pair), BF16)
    for s in chunks:
        x_at, pair_at = chunk(ROWS, s)
        take = pl.ds(pl.multiple_of((x_at * 2 + pair_at) * 128, 128), 128)
        by_expert = jnp.zeros((8, pair), F32)
        for j in range(LINE):
            tile_j = score_r[j, :, take]
            for e in range(2):
                block = e * LINE + j
                mine = jnp.where(row == block, tile_j, 0.0).astype(BF16)
                hot = jnp.concatenate([sel_s[ROWS, s, block * slot : (block + 1) * slot, :], pad], axis=0)
                by_expert = by_expert + jnp.dot(mine, hot, preferred_element_type=F32)
        for m in range(2):
            i, q = 2 * (s % 2) + m, s // 2
            ids = metas[meta_at(ROWS, member(ROWS, i), x_at), 0:8]
            mine = jnp.where(lax.rem(z + m, 2) == 0, by_expert[:, :tok], by_expert[:, tok:])
            total = jnp.zeros((8, tok), F32)
            for block in range(8):
                total = total + jnp.where(ids == numbers[block : block + 1], mine[block : block + 1], 0.0)
            cg_s[2 * i + q] = total
            if (i, q) != (0, 0):
                cg_copy(i, q).start()

    for p in paths:
        drain(far.at[p], far_recv.at[p])
        for d in range(2):
            mid = partial_at(p, wrap(line[p] + 1 - 2 * d), xh, d)
            mid[...] = (mid[...].astype(F32) + far[p, d].astype(F32)).astype(BF16)
            rs_copy(p, d, 2).start()
    for p in paths:
        drain(near.at[p, 0], rs_recv.at[p, 0])
        sum_up(p, 0)
        fin_copy(p, 0).start()

    drain(cg_r, cg_recv)
    total = cg_s[0]
    for i in range(len(others)):
        total = total + cg_r[i]
    cg_ref[...] = total.astype(BF16)
    drain(final, fin_recv)
    for p in paths:
        out_ref[:, pl.ds(p * cols, cols)] = (final[0, p].astype(F32) + final[1, p].astype(F32)).astype(BF16)

    drain(blocks.at[pl.ds(0, 6 * group), :], ret_send)
    drain(staged.at[pl.ds(0, 12 * tok), pl.ds(0, cols)], rs_send)
    drain(final, fin_send)
    drain(score_r.at[pl.ds(1, 3)], sc_send)
    drain(cg_r, cg_send)


def hand_on(grad_in, score_in, grad_out, score_out):
    grad_out[...] = grad_in[...]
    score_out[...] = score_in[...]


def on_device(layer_input, out_grad, expert_ids, combine, w_gate, w_up, w_down):
    tok, width = layer_input.shape[1:]
    hidden_units = w_gate.shape[3]
    experts = w_gate.shape[1] * lax.axis_size("ep")
    cap = 3 * tok * expert_ids.shape[2] // (2 * experts)
    slot = 2 * cap
    per_expert = LINE * LINE * slot
    part_rows = per_expert // 2
    cols = width // 2
    vmem, hbm = pl.BlockSpec(memory_space=pltpu.VMEM), pl.BlockSpec(memory_space=pl.ANY)
    dma = pltpu.SemaphoreType.DMA
    grad, scores = pl.pallas_call(
        functools.partial(kernel, tok, cap, width, hidden_units),
        out_shape=(jax.ShapeDtypeStruct((tok, width), BF16), jax.ShapeDtypeStruct((8, tok), BF16)),
        in_specs=[hbm, hbm, vmem, vmem, hbm, hbm, hbm],
        out_specs=(vmem, vmem),
        scratch_shapes=[
            pltpu.VMEM((2 * LINE * 2 * tok, width), BF16),
            pltpu.VMEM((part_rows, width), BF16),
            pltpu.VMEM((2 * LINE * 2, 16, tok), F32),
            pltpu.VMEM((2 * 3 * 2 * LINE * slot, width), BF16),
            pltpu.VMEM((2 * 2 * per_expert, width), BF16),
            pltpu.VMEM((2, 2, LINE, 2, 2 * slot, cols), BF16),
            pltpu.VMEM((2, 2, 2, tok, cols), BF16),
            pltpu.VMEM((2, 2, tok // 2, cols), BF16),
            pltpu.VMEM((2, tok, cols), BF16),
            pltpu.VMEM((2, 2, tok, cols), BF16),
            pltpu.VMEM((2, LINE, 8 * slot, 2 * tok), BF16),
            pltpu.VMEM((2, LINE, 2 * tok, 8 * slot), BF16),
            pltpu.VMEM((width, hidden_units), BF16),
            pltpu.VMEM((width, hidden_units), BF16),
            pltpu.VMEM((hidden_units, width), BF16),
            pltpu.VMEM((part_rows, hidden_units), BF16),
            pltpu.VMEM((part_rows, hidden_units), BF16),
            pltpu.VMEM((per_expert, 128), F32),
            pltpu.VMEM((LINE, 8, LINE * 128), F32),
            pltpu.VMEM((part_rows, 128), F32),
            pltpu.VMEM((LINE, 8, LINE * 128), F32),
            pltpu.VMEM((LINE * 2, 8, tok), F32),
            pltpu.VMEM((LINE * 2 - 1, 8, tok), F32),
            dma, dma((2,)), dma((2, 2, 2)), dma((2, 2, 2)), dma((2, 2)), dma, dma, dma((2,)), dma((3,)),
            dma, dma((2, 2, 2)), dma, dma((2, 2)), dma((2, 2)), dma, dma, dma, dma,
            dma, dma((2, 2)), dma((2,)), dma((2,)), dma, dma,
        ],
        compiler_params=pltpu.CompilerParams(
            collective_id=0, has_side_effects=True, vmem_limit_bytes=63 << 20
        ),
        cost_estimate=pl.CostEstimate(
            flops=10 * 2 * per_expert * width * hidden_units, bytes_accessed=24 << 20, transcendentals=0
        ),
        name="routed_backward",
    )(layer_input[0], out_grad[0], expert_ids[0].T, combine[0].T, w_gate[0], w_up[0], w_down[0])
    grad, scores = pl.pallas_call(
        hand_on,
        out_shape=(jax.ShapeDtypeStruct((tok, width), BF16), jax.ShapeDtypeStruct((8, tok), BF16)),
        in_specs=[vmem, vmem],
        out_specs=(vmem, vmem),
        name="results",
    )(grad, scores)
    return grad[None], scores.T[None]


def solution(mesh):
    return jax.shard_map(
        on_device,
        mesh=mesh,
        in_specs=(
            P("pp", "ep", None),
            P("pp", "ep", None),
            P("pp", "ep", None),
            P("pp", "ep", None),
            P("pp", "ep", None, None),
            P("pp", "ep", None, None),
            P("pp", "ep", None, None),
        ),
        out_specs=(P("pp", "ep", None), P("pp", "ep", None)),
        check_vma=False,
    )
```

```python
import functools

import jax
import jax.numpy as jnp
from jax import lax
from jax.experimental import pallas as pl
from jax.experimental.pallas import tpu as pltpu
from jax.sharding import PartitionSpec as P

MESH = pl.DeviceIdType.MESH
LINE = 4
BF16 = jnp.bfloat16
F32 = jnp.float32
ROWS, GRADS = 0, 1


def kernel(
    tok, cap, width, hidden_units,
    rows_in, grads_in, ids_in, share_in, gate_w, up_w, down_w,
    out_ref, cg_ref,
    blocks, early, metas, staged, arrived, returned, near, near_own, far, beside, final,
    sel_s, wsel_s, wg, wu, wd, gg_s, ug_s, score_0, score_s, score_acc, score_r, cg_s, cg_r,
    block_send, x_recv, xn_recv, ag_recv, ag_far, meta_send, meta_recv, own_sem, w_sem,
    fwd_send, fwd_recv, ret_send, ret_recv, sc_send, sc_recv, cg_send, cg_recv,
    rs_send, rs_recv, near_recv, far_recv, beside_recv, fin_send, fin_recv,
):
    slot = 2 * cap
    group = LINE * slot
    half = tok // 2
    cols = width // 2
    pair = 2 * tok
    per_expert = LINE * group
    part_rows = per_expert // 2
    pp, ep = lax.axis_index("pp"), lax.axis_index("ep")
    z, xh, y = ep // 8, (ep // 4) % 2, ep % 4
    line, cross = (z, y), (y, z)
    inputs = (rows_in, grads_in)

    def wrap(v):
        return lax.rem(v + LINE, LINE)

    def member(p, i):
        c = line[p]
        return (c, (c // 2) * 2 + 1 - c % 2, wrap(c + 2), 3 - c)[i]

    def column(q):
        return xh if q == 0 else 1 - xh

    def chunk(p, s):
        at = line[p] // 2 if s % 2 == 0 else 1 - line[p] // 2
        return column(s // 2), at

    chunks = range(4)

    def device(p, line_at, x_at, cross_at, section=None):
        z_at, y_at = (line_at, cross_at) if p == ROWS else (cross_at, line_at)
        return {"pp": pp if section is None else section, "ep": z_at * 8 + x_at * 4 + y_at}

    def remote(src, dst, send, recv, to):
        return pltpu.make_async_remote_copy(
            src_ref=src, dst_ref=dst, send_sem=send, recv_sem=recv, device_id=to, device_id_type=MESH
        )

    def drain(ref, sem):
        pltpu.make_async_copy(ref, ref, sem).wait()

    def meta_at(p, line_at, x_at):
        return (p * LINE + line_at) * 2 + x_at

    def place(p, line_at, x_at, part=None):
        start = ((p * 2 + x_at) * LINE + line_at) * tok
        if part is None:
            return blocks.at[pl.ds(pl.multiple_of(start, tok), tok), :]
        return blocks.at[pl.ds(pl.multiple_of(start + part * half, half), half), :]

    before, after = lax.rem(pp + 3, 4), lax.rem(pp + 1, 4)
    peers = [device(ROWS, member(ROWS, i), column(q), y) for i in range(LINE) for q in range(2)][1:]
    peers += [device(GRADS, member(GRADS, i), column(q), z) for i in range(1, LINE) for q in range(2)]
    peers += [device(ROWS, z, x_at, y, s) for x_at in (xh, 1 - xh) for s in (before, after)]
    barrier = pltpu.get_barrier_semaphore()
    for peer in peers:
        pl.semaphore_signal(barrier, inc=1, device_id=peer, device_id_type=MESH)

    def own_half(p, part):
        return inputs[p].at[pl.ds(pl.multiple_of(part * half, half), half), :]

    def x_copy(p, part):
        return remote(
            own_half(p, part), place(p, line[p], xh, part), block_send, x_recv.at[p],
            device(p, line[p], 1 - xh, cross[p]),
        )

    def x_wait(p):
        drain(place(p, line[p], 1 - xh), x_recv.at[p])

    def xn_copy(p, d, k):
        dst = place(p, wrap(line[p] - (1 - 2 * d)), xh, ag_part(d, k))
        return remote(dst, dst, block_send, xn_recv.at[p, d, k], device(p, line[p], 1 - xh, cross[p]))

    def xn_wait(p, d, k):
        drain(place(p, wrap(line[p] - (1 - 2 * d)), 1 - xh, ag_part(d, k)), xn_recv.at[p, d, k])

    def ag_part(d, k):
        return lax.rem(d + k, 2) if k < 2 else d

    def ag_copy(p, q, d, k):
        step = 1 - 2 * d
        part = ag_part(d, k)
        x_at = xh if q == 0 else 1 - xh
        at = line[p] if k < 2 else wrap(line[p] - step)
        dst = place(p, at, x_at, part)
        src = own_half(p, part) if q == 0 and k < 2 else dst
        sem = ag_recv.at[p, d, k] if k < 2 else ag_far.at[p, q]
        return remote(src, dst, block_send, sem, device(p, wrap(line[p] + step), xh, cross[p]))

    def ag_wait(p, d, k):
        drain(place(p, wrap(line[p] - (1 - 2 * d)), xh, ag_part(d, k)), ag_recv.at[p, d, k])

    def ag_wait_far(p, q):
        drain(place(p, wrap(line[p] + 2), column(q)), ag_far.at[p, q])

    def meta_copy(p, i, q):
        mine = metas.at[meta_at(p, line[p], xh)]
        return remote(mine, mine, meta_send, meta_recv, device(p, member(p, i), column(q), cross[p]))

    others = [(i, q) for i in range(LINE) for q in range(2) if (i, q) != (0, 0)]
    paths = (ROWS, GRADS)
    def in_weights(e):
        return [pltpu.make_async_copy(src.at[e], dst.at[e], w_sem.at[e]) for src, dst in ((gate_w, wg), (up_w, wu))]

    def out_weights(e):
        return [pltpu.make_async_copy(down_w.at[e], wd, w_sem.at[2])]

    own = []
    for p in paths:
        own.append(pltpu.make_async_copy(inputs[p], place(p, line[p], xh), own_sem.at[p]))
        own[-1].start()

    for copy in in_weights(0) + out_weights(0) + in_weights(1):
        copy.start()
    for p in paths:
        metas[meta_at(p, line[p], xh), 0:8] = ids_in[...].astype(F32)
        metas[meta_at(p, line[p], xh), 8:16] = share_in[...]
    pl.semaphore_wait(barrier, len(peers))
    for p in paths:
        for i, q in others:
            meta_copy(p, i, q).start()
    for p in paths:
        for part in range(2):
            x_copy(p, part).start()
    for k in range(2):
        for p in paths:
            for d in range(2):
                ag_copy(p, 0, d, k).start()
    def wait_weights(e):
        drain(wg, w_sem.at[e])
        out_weights(e)[0].wait()

    all_metas = metas.at[pl.ds(0, 2 * len(others))]
    drain(all_metas, meta_recv)

    def expert_numbers(p):
        row = lax.broadcasted_iota(jnp.int32, (8, tok), 0)
        e, across = row // LINE, (row + cross[p]) % LINE
        if p == ROWS:
            return 16 * z + 8 * xh + 2 * across + e
        return 16 * across + 8 * xh + 2 * y + e

    earlier = (
        lax.broadcasted_iota(jnp.int32, (tok, tok), 0) < lax.broadcasted_iota(jnp.int32, (tok, tok), 1)
    ).astype(F32).astype(BF16)
    rank_no = lax.broadcasted_iota(jnp.int32, (cap, tok), 0).astype(F32)
    nothing = jnp.zeros((cap, tok), F32)

    for p in paths:
        numbers = expert_numbers(p).astype(F32)

        def build(i, carry, p=p, numbers=numbers):
            x_at = lax.rem(xh + i // 2, 2)
            own_pair = line[p] // 2
            first_line = 2 * lax.rem(own_pair + i % 2, 2)
            weight, rank = [], []
            for h in range(2):
                meta = metas[meta_at(p, first_line + h, x_at)]
                named = jnp.zeros((8, tok), F32)
                share = jnp.zeros((8, tok), F32)
                for k in range(8):
                    same = meta[k : k + 1, :] == numbers
                    named = named + jnp.where(same, 1.0, 0.0)
                    share = share + jnp.where(same, meta[8 + k : 9 + k, :], 0.0)
                before_it = jnp.dot(named.astype(BF16), earlier, preferred_element_type=F32)
                rank.append(jnp.where(named > 0.0, before_it, -1.0))
                weight.append(share)
            hot, hot_w = [], []
            for row in range(8):
                for h in range(2):
                    hit = rank[h][row : row + 1, :] == rank_no
                    one = jnp.where(hit, 1.0, 0.0)
                    scaled = jnp.where(hit, weight[h][row : row + 1, :], 0.0)
                    hot.append(jnp.concatenate([one, nothing] if h == 0 else [nothing, one], axis=1))
                    hot_w.append(jnp.concatenate([scaled, nothing] if h == 0 else [nothing, scaled], axis=1))
            sel_s[p, i] = jnp.concatenate(hot, axis=0).astype(BF16)
            wsel_s[p, i] = jnp.concatenate(hot_w, axis=0).T.astype(BF16)
            return carry

        lax.fori_loop(0, LINE, build, 0)

    def arrived_at(p, e, from_cross, x_at, pair_at):
        start = (p * 2 + e) * per_expert + ((x_at * LINE + from_cross) * 2 + pair_at) * slot
        return arrived.at[pl.ds(pl.multiple_of(start, 16), slot), :]

    def fwd_copy(p, e, j, s):
        return remote(
            staged.at[pl.ds((((p * 3 + j - 1) * 2 + e) * 4 + s) * slot, slot), :],
            arrived_at(p, e, cross[p], *chunk(p, s)), fwd_send, fwd_recv.at[p, e, s // 2],
            device(p, line[p], xh, wrap(cross[p] + j)),
        )

    tile = 512

    def select(p, s):
        x_at, pair_at = chunk(p, s)
        start = pl.multiple_of(((p * 2 + x_at) * 2 + pair_at) * pair, pair)

        @pl.loop(0, width // tile)
        def _(n):
            lanes = pl.ds(pl.multiple_of(n * tile, tile), tile)
            picked = jnp.dot(
                sel_s[p, s], blocks[pl.ds(start, pair), lanes], preferred_element_type=F32
            ).astype(BF16)
            for e in range(2):
                for j in range(LINE):
                    part = picked[(e * LINE + j) * slot : (e * LINE + j + 1) * slot]
                    if j == 0:
                        arrived_at(p, e, cross[p], x_at, pair_at)[:, lanes] = part
                    else:
                        first = (((p * 3 + j - 1) * 2 + e) * 4 + s) * slot
                        staged[pl.ds(first, slot), lanes] = part

    far_first = (2, 1, 3)

    def send_selected(p, e, s):
        for j in far_first:
            fwd_copy(p, e, j, s).start()

    def grad_rows(p, e, q, size, start):
        if (e, q) == (0, 0):
            return early.at[pl.ds(start, size), pl.ds(p * cols, cols)]
        base = {(0, 1): 0, (1, 1): 1, (1, 0): 2}[e, q] * part_rows
        return blocks.at[pl.ds(pl.multiple_of(base + start, 16), size), pl.ds(p * cols, cols)]

    def grads_for(p, e, q, j):
        return grad_rows(p, e, q, group // 2, pl.multiple_of(wrap(cross[p] + j) * (group // 2), 16))

    def ret_copy(p, e, j, q):
        return remote(
            grads_for(p, e, q, j), returned.at[p, q, LINE - j - 1, e], ret_send, ret_recv.at[p, q],
            device(p, line[p], xh, wrap(cross[p] + j)),
        )

    transposed = (((1,), (1,)), ((), ()))
    f_tile = 256
    d_tile = 256
    low = lax.broadcasted_iota(jnp.int32, (part_rows, 128), 1) < 64

    def turn(value):
        blocks_of = [value[(a * LINE + b) * cap : (a * LINE + b + 1) * cap] for b in range(LINE) for a in range(LINE)]
        return jnp.concatenate(blocks_of, axis=0)

    def expert(e, q):
        for p in paths:
            drain(arrived.at[pl.ds((p * 2 + e) * per_expert, 3 * group // 2), :], fwd_recv.at[p, e, q])
        offset = column(q) * part_rows
        row_at = pl.ds(pl.multiple_of(e * per_expert + offset, part_rows), part_rows)
        grad_at = pl.ds(pl.multiple_of((2 + e) * per_expert + offset, part_rows), part_rows)

        @pl.loop(0, hidden_units // f_tile)
        def _(n):
            units = pl.ds(pl.multiple_of(n * f_tile, f_tile), f_tile)
            gate = jnp.dot(arrived[row_at, :], wg[e, :, units], preferred_element_type=F32)
            up = jnp.dot(arrived[row_at, :], wu[e, :, units], preferred_element_type=F32)
            back = lax.dot_general(arrived[grad_at, :], wd[units, :], transposed, preferred_element_type=F32)
            back = turn(back)
            sigma = jax.nn.sigmoid(gate)
            active = gate * sigma
            hidden = (active * up).astype(BF16).astype(F32)
            term = hidden * back
            gg_s[:, units] = (back * up * sigma * (1.0 + gate * (1.0 - sigma))).astype(BF16)
            ug_s[:, units] = (back * active).astype(BF16)
            term = term[:, :128] + term[:, 128:]

            @pl.when(n == 0)
            def _():
                score_acc[...] = term

            @pl.when(n > 0)
            def _():
                score_acc[...] += term

        if (e, q) == (0, 1):
            out_weights(1)[0].start()
        for p in paths:

            @pl.loop(0, cols // d_tile)
            def _(n, p=p):
                lanes = pl.ds(pl.multiple_of(p * cols + n * d_tile, d_tile), d_tile)
                grad = lax.dot_general(gg_s[...], wg[e, lanes, :], transposed, preferred_element_type=F32)
                grad = grad + lax.dot_general(ug_s[...], wu[e, lanes, :], transposed, preferred_element_type=F32)
                grad = (grad if p == ROWS else turn(grad)).astype(BF16)
                grad_rows(p, e, q, part_rows, 0)[:, pl.ds(pl.multiple_of(n * d_tile, d_tile), d_tile)] = grad

            for j in far_first:
                ret_copy(p, e, j, q).start()

        score = jnp.broadcast_to(jnp.sum(score_acc[...], axis=1, keepdims=True), (part_rows, 128))
        rows = pl.ds(pl.multiple_of(offset, part_rows), part_rows)
        if e == 0:
            score_0[rows, :] = score
        else:
            score_0[rows, :] = jnp.where(low, score_0[rows, :], score)

    near_way = [1 - line[p] % 2 for p in paths]
    far_way = [line[p] % 2 for p in paths]
    for p in paths:
        ag_wait(p, near_way[p], 0)
        ag_copy(p, 0, near_way[p], 2).start()
        xn_copy(p, near_way[p], 0).start()
        ag_wait(p, far_way[p], 0)
        ag_copy(p, 0, far_way[p], 2).start()
    for p in paths:
        ag_wait(p, near_way[p], 1)
        xn_copy(p, near_way[p], 1).start()
        own[p].wait()
        select(p, 0)
        send_selected(p, 0, 0)
    for p in paths:
        ag_wait(p, far_way[p], 1)
        ag_wait_far(p, 0)
        select(p, 1)
        send_selected(p, 0, 1)
    for s in (0, 1):
        for p in paths:
            send_selected(p, 1, s)
    for p in paths:
        x_wait(p)
        for k in range(2):
            xn_copy(p, far_way[p], k).start()
    wait_weights(0)
    expert(0, 0)
    for p in paths:
        xn_wait(p, near_way[p], 0)
        ag_copy(p, 1, near_way[p], 2).start()
        xn_wait(p, near_way[p], 1)
        select(p, 2)
        send_selected(p, 0, 2)
    for p in paths:
        xn_wait(p, far_way[p], 0)
        ag_copy(p, 1, far_way[p], 2).start()
    for p in paths:
        xn_wait(p, far_way[p], 1)
        ag_wait_far(p, 1)
        select(p, 3)
        send_selected(p, 0, 3)
    for s in (2, 3):
        for p in paths:
            send_selected(p, 1, s)
    drain(blocks.at[pl.ds(0, 14 * tok), :], block_send)
    drain(all_metas, meta_send)

    def score_copy(j):
        return remote(
            score_s.at[wrap(y + j)], score_r.at[LINE - j], sc_send, sc_recv,
            device(ROWS, z, xh, wrap(y + j)),
        )

    expert(0, 1)
    wait_weights(1)
    expert(1, 1)
    expert(1, 0)
    drain(staged, fwd_send)

    def partial_at(p, at, x_at, part=None, h=None):
        start = (x_at * LINE + at) * tok
        lanes = pl.ds(p * cols, cols) if h is None else pl.ds(p * cols + h * (cols // 2), cols // 2)
        if part is None:
            return staged.at[pl.ds(pl.multiple_of(start, tok), tok), lanes]
        return staged.at[pl.ds(pl.multiple_of(start + part * half, half), half), lanes]

    def combine(p, s):
        x_at, pair_at = chunk(p, s)
        take = pl.ds(pl.multiple_of(pair_at * slot, 16), slot)
        parts = []
        for e in range(2):
            parts.append(grads_for(p, e, s // 2, 0)[take, :])
            parts += [returned[p, s // 2, j - 1, e, take, :] for j in range(1, LINE)]
        gathered = jnp.concatenate(parts, axis=0)
        rows = pl.ds(pl.multiple_of((x_at * 2 + pair_at) * pair, pair), pair)
        for n in range(cols // tile):
            staged[rows, pl.ds(p * cols + n * tile, tile)] = jnp.dot(
                wsel_s[p, s], gathered[:, n * tile : (n + 1) * tile], preferred_element_type=F32
            ).astype(BF16)

    def rs_copy(p, d, k, h=None):
        step = 1 - 2 * d
        at = wrap(line[p] + 2) if k == 0 else wrap(line[p] + step)
        part = 1 - d if k == 1 else d
        dst = far.at[p, d] if k == 0 else near_own.at[p, h, d, pl.ds(pl.multiple_of(part * half, half), half)]
        return remote(
            partial_at(p, at, xh, part, h), dst, rs_send, far_recv.at[p] if k == 0 else near_recv.at[p, h],
            device(p, wrap(line[p] + step), xh, cross[p]),
        )

    def rs_whole(p, d):
        step = 1 - 2 * d
        return remote(
            partial_at(p, wrap(line[p] + step), 1 - xh), near.at[p, d], rs_send, rs_recv.at[p],
            device(p, wrap(line[p] + step), xh, cross[p]),
        )

    def beside_copy(p):
        return remote(
            partial_at(p, wrap(line[p] + 2), 1 - xh), beside.at[p], rs_send, beside_recv.at[p],
            device(p, line[p], 1 - xh, cross[p]),
        )

    def fin_copy(p, q, h=None):
        lanes = pl.ds(0, cols) if h is None else pl.ds(h * (cols // 2), cols // 2)
        return remote(
            partial_at(p, line[p], column(q), None, h), final.at[q, p, :, lanes], fin_send, fin_recv,
            device(p, line[p], column(q), cross[p], before),
        )

    def cg_copy(i, q):
        return remote(
            cg_s.at[2 * i + q], cg_r.at[2 * i + q - 1], cg_send, cg_recv,
            device(ROWS, member(ROWS, i), column(q), y),
        )

    def sum_up(mine, others):
        mine[...] = (mine[...].astype(F32) + others[0].astype(F32) + others[1].astype(F32)).astype(BF16)

    def wait_returned(p, q):
        drain(returned.at[p, q], ret_recv.at[p, q])

    for p in paths:
        wait_returned(p, 1)
        combine(p, 3)
        beside_copy(p).start()
        rs_whole(p, near_way[p]).start()
        combine(p, 2)
        rs_whole(p, far_way[p]).start()
    blank = jnp.zeros((128 - slot, 128), F32)
    first = lax.broadcasted_iota(jnp.int32, (8, 128), 0) < 4
    for y_src in range(LINE):
        for t in range(4):
            start = ((t // 2 * LINE + y_src) * 2 + t % 2) * slot
            turned = jnp.concatenate([score_0[start : start + slot, :], blank], axis=0).T
            score_s[y_src, :, t * 128 : (t + 1) * 128] = jnp.where(first, turned[0:8], turned[64:72])
    for j in far_first:
        score_copy(j).start()
    score_r[0] = score_s[y]
    for p in paths:
        wait_returned(p, 0)
        combine(p, 1)
    for p in paths:
        drain(beside.at[p], beside_recv.at[p])
        mine = partial_at(p, wrap(line[p] + 2), xh)
        mine[...] = (mine[...].astype(F32) + beside[p].astype(F32)).astype(BF16)
        for d in range(2):
            rs_copy(p, d, 0).start()
        for h in range(2):
            rs_copy(p, near_way[p], 1, h).start()
    for p in paths:
        combine(p, 0)
        for h in range(2):
            rs_copy(p, far_way[p], 1, h).start()
    for p in paths:
        drain(near.at[p], rs_recv.at[p])
        sum_up(partial_at(p, line[p], 1 - xh), near[p])
        fin_copy(p, 1).start()

    drain(score_r.at[pl.ds(1, 3)], sc_recv)
    row = lax.broadcasted_iota(jnp.int32, (8, 128), 0)
    numbers = expert_numbers(ROWS).astype(F32)
    pad = jnp.zeros((128 - slot, pair), BF16)
    def score_chunk(s):
        x_at, pair_at = chunk(ROWS, s)
        take = pl.ds(pl.multiple_of((x_at * 2 + pair_at) * 128, 128), 128)
        by_expert = jnp.zeros((8, pair), F32)
        for j in range(LINE):
            tile_j = score_r[j, :, take]
            for e in range(2):
                block = e * LINE + j
                mine = jnp.where(row == block, tile_j, 0.0).astype(BF16)
                hot = jnp.concatenate([sel_s[ROWS, s, block * slot : (block + 1) * slot, :], pad], axis=0)
                by_expert = by_expert + jnp.dot(mine, hot, preferred_element_type=F32)
        for m in range(2):
            i, q = 2 * (s % 2) + m, s // 2
            ids = metas[meta_at(ROWS, member(ROWS, i), x_at), 0:8]
            mine = jnp.where(lax.rem(z + m, 2) == 0, by_expert[:, :tok], by_expert[:, tok:])
            total = jnp.zeros((8, tok), F32)
            for block in range(8):
                total = total + jnp.where(ids == numbers[block : block + 1], mine[block : block + 1], 0.0)
            cg_s[2 * i + q] = total
            if (i, q) != (0, 0):
                cg_copy(i, q).start()

    for s in (0, 1):
        score_chunk(s)
    for p in paths:
        drain(far.at[p], far_recv.at[p])
        for d in range(2):
            mid = partial_at(p, wrap(line[p] + 1 - 2 * d), xh, d)
            mid[...] = (mid[...].astype(F32) + far[p, d].astype(F32)).astype(BF16)
            rs_copy(p, d, 2, 0).start()
    for p in paths:
        for d in range(2):
            rs_copy(p, d, 2, 1).start()
    for s in (2, 3):
        score_chunk(s)
    for h in range(2):
        for p in paths:
            drain(near_own.at[p, h], near_recv.at[p, h])
            sum_up(partial_at(p, line[p], xh, None, h), near_own[p, h])
            fin_copy(p, 0, h).start()

    drain(cg_r, cg_recv)
    total = cg_s[0]
    for i in range(len(others)):
        total = total + cg_r[i]
    cg_ref[...] = total.astype(BF16)
    drain(final, fin_recv)
    for p in paths:
        out_ref[:, pl.ds(p * cols, cols)] = (final[0, p].astype(F32) + final[1, p].astype(F32)).astype(BF16)

    drain(blocks.at[pl.ds(0, 6 * group), :], ret_send)
    drain(staged.at[pl.ds(0, 12 * tok), pl.ds(0, cols)], rs_send)
    drain(final, fin_send)
    drain(score_r.at[pl.ds(1, 3)], sc_send)
    drain(cg_r, cg_send)


def hand_on(grad_in, score_in, grad_out, score_out):
    grad_out[...] = grad_in[...]
    score_out[...] = score_in[...]


def on_device(layer_input, out_grad, expert_ids, combine, w_gate, w_up, w_down):
    tok, width = layer_input.shape[1:]
    hidden_units = w_gate.shape[3]
    experts = w_gate.shape[1] * lax.axis_size("ep")
    cap = 3 * tok * expert_ids.shape[2] // (2 * experts)
    slot = 2 * cap
    per_expert = LINE * LINE * slot
    part_rows = per_expert // 2
    cols = width // 2
    vmem, hbm = pl.BlockSpec(memory_space=pltpu.VMEM), pl.BlockSpec(memory_space=pl.ANY)
    dma = pltpu.SemaphoreType.DMA
    grad, scores = pl.pallas_call(
        functools.partial(kernel, tok, cap, width, hidden_units),
        out_shape=(jax.ShapeDtypeStruct((tok, width), BF16), jax.ShapeDtypeStruct((8, tok), BF16)),
        in_specs=[hbm, hbm, vmem, vmem, hbm, hbm, hbm],
        out_specs=(vmem, vmem),
        scratch_shapes=[
            pltpu.VMEM((2 * LINE * 2 * tok, width), BF16),
            pltpu.VMEM((part_rows, width), BF16),
            pltpu.VMEM((2 * LINE * 2, 16, tok), F32),
            pltpu.VMEM((2 * 3 * 2 * LINE * slot, width), BF16),
            pltpu.VMEM((2 * 2 * per_expert, width), BF16),
            pltpu.VMEM((2, 2, LINE - 1, 2, 2 * slot, cols), BF16),
            pltpu.VMEM((2, 2, tok, cols), BF16),
            pltpu.VMEM((2, 2, 2, tok, cols // 2), BF16),
            pltpu.VMEM((2, 2, tok // 2, cols), BF16),
            pltpu.VMEM((2, tok, cols), BF16),
            pltpu.VMEM((2, 2, tok, cols), BF16),
            pltpu.VMEM((2, LINE, 8 * slot, 2 * tok), BF16),
            pltpu.VMEM((2, LINE, 2 * tok, 8 * slot), BF16),
            pltpu.VMEM((2, width, hidden_units), BF16),
            pltpu.VMEM((2, width, hidden_units), BF16),
            pltpu.VMEM((hidden_units, width), BF16),
            pltpu.VMEM((part_rows, hidden_units), BF16),
            pltpu.VMEM((part_rows, hidden_units), BF16),
            pltpu.VMEM((per_expert, 128), F32),
            pltpu.VMEM((LINE, 8, LINE * 128), F32),
            pltpu.VMEM((part_rows, 128), F32),
            pltpu.VMEM((LINE, 8, LINE * 128), F32),
            pltpu.VMEM((LINE * 2, 8, tok), F32),
            pltpu.VMEM((LINE * 2 - 1, 8, tok), F32),
            dma, dma((2,)), dma((2, 2, 2)), dma((2, 2, 2)), dma((2, 2)), dma, dma, dma((2,)), dma((3,)),
            dma, dma((2, 2, 2)), dma, dma((2, 2)), dma, dma, dma, dma,
            dma, dma((2,)), dma((2, 2)), dma((2,)), dma((2,)), dma, dma,
        ],
        compiler_params=pltpu.CompilerParams(
            collective_id=0, has_side_effects=True, vmem_limit_bytes=63 << 20
        ),
        cost_estimate=pl.CostEstimate(
            flops=10 * 2 * per_expert * width * hidden_units, bytes_accessed=24 << 20, transcendentals=0
        ),
        name="routed_backward",
    )(layer_input[0], out_grad[0], expert_ids[0].T, combine[0].T, w_gate[0], w_up[0], w_down[0])
    grad, scores = pl.pallas_call(
        hand_on,
        out_shape=(jax.ShapeDtypeStruct((tok, width), BF16), jax.ShapeDtypeStruct((8, tok), BF16)),
        in_specs=[vmem, vmem],
        out_specs=(vmem, vmem),
        name="results",
    )(grad, scores)
    return grad[None], scores.T[None]


def solution(mesh):
    return jax.shard_map(
        on_device,
        mesh=mesh,
        in_specs=(
            P("pp", "ep", None),
            P("pp", "ep", None),
            P("pp", "ep", None),
            P("pp", "ep", None),
            P("pp", "ep", None, None),
            P("pp", "ep", None, None),
            P("pp", "ep", None, None),
        ),
        out_specs=(P("pp", "ep", None), P("pp", "ep", None)),
        check_vma=False,
    )
```
